256 devices in a mesh: member: 4 (over y), grid: 16 (over z_lo, x, core), dp: 4 (over z_hi).
Axes of the slice: x: 4, y: 4, z: 8 (z_hi: 4, z_lo: 2; z = z_hi * 2 + z_lo), core: 2. Of those that a mesh axis runs over, the one named last changes fastest.
Arguments:
- latents: bfloat16 [4, 16, 4096, 1024], P('dp', 'member', 'grid'), may hold values from -10 to 10
- w_in: bfloat16 [1024, 1024], replicated, may hold values from -0.1875 to 0.1875
- b_in: float32 [1024], replicated, may hold values from -4 to 4
- w_out: bfloat16 [1024, 100], replicated, may hold values from -0.1875 to 0.1875
- b_out: float32 [100], replicated, may hold values from -4 to 4
- targets: float32 [4, 100, 4096], P('dp', None, ('grid', 'member')), may hold values from -6 to 6
- area: float32 [4096], P(('grid', 'member')), may hold values from 0.3 to 9
- var_weight: float32 [100], replicated, may hold values from 0.3 to 3
- member_rank: int32 [4, 16, 100, 4096], P('dp', None, None, ('grid', 'member')), may hold values from 0 to 15, as said below
- obs_rank: int32 [4, 100, 4096], P('dp', None, ('grid', 'member')), may hold values from 0 to 16
Outputs:
- loss: float32 [4], P('dp')
- grad_w_in: float32 [1024, 1024], P(('member', 'grid', 'dp'))
- grad_w_out: float32 [1024, 100], replicated
- grad_b_in: float32 [1024], replicated
- grad_b_out: float32 [100], replicated
The draws below stay inside these ranges and needn't reach their ends.
Inputs may be any that keep to these rules, and one draw needn't show every extreme that they name: For each sample, variable and point, member_rank over the 16 members is a permutation of 0 to 15.
All inputs are finite; a program needn't handle non-finite values.
Results may differ from the reference program's by a relative error of at most 0.0031.
Values may be sent and summed in bfloat16 or wider, within the bound.
No kernel may reach another device: no remote copies, remote signals or barrier semaphores. Data moves between devices by JAX's collectives and lax.ppermute only.
A program may use at most 64 MiB of HBM per device.

```python
import math
import jax
import jax.numpy as jnp
from jax import lax

LAT = 1024
HID = 1024
VARS = 100
MEM_DEV = 4
MEMBERS = 16
POINTS = 4096
SAMPLES = 4


def draw_latents(key, part):
    key = jax.random.fold_in(key, 37)
    scale_key, common_key, member_key = jax.random.split(key, 3)
    groups = MEMBERS // MEM_DEV
    lower_end = 0.2
    upper_end = 1.5
    own_scale = 0.6
    shared = jnp.exp(jax.random.uniform(scale_key, (SAMPLES, groups, 1, 1, 1), jnp.float32, math.log(lower_end), math.log(upper_end)))
    common = jax.random.normal(common_key, (SAMPLES, groups, 1, POINTS, LAT), jnp.float32)
    personal = jax.random.normal(member_key, (SAMPLES, groups, MEM_DEV, POINTS, LAT), jnp.float32)
    mixture = shared * common + own_scale * personal
    mixture = jnp.clip(mixture, -10.0, 10.0)
    return mixture.reshape(SAMPLES, MEMBERS, POINTS, LAT).astype(jnp.bfloat16)


def draw_area(key, part):
    key = jax.random.fold_in(key, 11)
    rising = 1.0 + 2.0 * jnp.arange(POINTS, dtype=jnp.float32) / POINTS
    base = jnp.exp(jax.random.uniform(key, (POINTS,), jnp.float32, jnp.log(0.5), jnp.log(2.0)))
    return (rising * base).astype(jnp.float32)


def draw_member_rank(key, part):
    key = jax.random.fold_in(key, 23)
    scores = jax.random.randint(key, (SAMPLES, MEMBERS, VARS, POINTS), 0, 2 ** 20) * MEMBERS
    scores = scores + jnp.arange(MEMBERS, dtype=jnp.int32)[None, :, None, None]
    order = jnp.argsort(scores, axis=1, stable=True)
    return jnp.argsort(order, axis=1, stable=True).astype(jnp.int32)


def place_ends(result, rng, smallest, top_value):
    index_at = [jax.random.randint(jax.random.fold_in(rng, axis), (), 0, length) for axis, length in enumerate(result.shape)]
    main_axis = result.shape.index(max(result.shape))
    next_to = index_at[:main_axis] + [(index_at[main_axis] + 1) % result.shape[main_axis]] + index_at[main_axis + 1:]
    return result.at[tuple(index_at)].set(smallest).at[tuple(next_to)].set(top_value)


def block_levels(own_key, extent, pieces, smallest, largest):
    gain, own = 1.0, jax.random.fold_in(own_key, 6)
    for dim, shards_of in pieces:
        draws = jnp.exp(jax.random.uniform(jax.random.fold_in(own, dim), (shards_of,), jnp.float32, smallest / len(pieces), largest / len(pieces)))
        gain = gain * jnp.repeat(draws, extent[dim] // shards_of).reshape([-1 if axis == dim else 1 for axis in range(len(extent))])
    return gain


def noise(rng, dims, width, bound, cuts=(), held_as=jnp.bfloat16):
    level = block_levels(rng, dims, cuts, -0.22, 0.18) if cuts else 1.0
    values = jax.random.normal(rng, dims, jnp.float32) * width * level
    return jnp.minimum(jnp.maximum(values, -bound), bound).astype(held_as)


def setup_inputs(seed: int = 0) -> dict:
    seeds = jax.random.split(jax.random.key(seed), 11)
    latents = draw_latents(jax.random.fold_in(seeds[10], 71), 0)
    w_in = noise(seeds[1], (LAT, HID), LAT ** -0.5, 0.1875)
    b_in = noise(seeds[2], (HID,), 0.7, 4.0, (), jnp.float32)
    w_out = noise(seeds[3], (HID, VARS), HID ** -0.5, 0.1875)
    b_out = noise(seeds[4], (VARS,), 1.0, 4.0, (), jnp.float32)
    targets = noise(seeds[5], (SAMPLES, VARS, POINTS), 1.0, 6.0, ((0, 4), (2, 64)), jnp.float32)
    area = draw_area(jax.random.fold_in(seeds[10], 71), 0)
    var_weight = jnp.clip(jnp.exp(jax.random.uniform(seeds[7], (VARS,), jnp.float32, math.log(0.3), math.log(3.0))), 0.3, 3.0)
    member_rank = draw_member_rank(jax.random.fold_in(seeds[10], 71), 0)
    obs_rank = place_ends(jax.random.randint(seeds[9], (SAMPLES, VARS, POINTS), 0, MEMBERS + 1), jax.random.fold_in(seeds[9], 1), 0, MEMBERS).astype(jnp.int32)
    return {"latents": latents, "w_in": w_in, "b_in": b_in, "w_out": w_out, "b_out": b_out, "targets": targets, "area": area, "var_weight": var_weight, "member_rank": member_rank, "obs_rank": obs_rank}


ALPHA = 0.95

def reference(latents, w_in, b_in, w_out, b_out, targets, area, var_weight, member_rank, obs_rank):
    n_samp = latents.shape[0]
    n_mem = latents.shape[1]
    n_pts = latents.shape[2]
    n_vars = w_out.shape[1]
    blocks = latents.reshape(n_samp * n_mem, n_pts, latents.shape[3])

    def forward(rows):
        pre = jnp.dot(rows, w_in, preferred_element_type=jnp.float32) + b_in
        hidden = jax.nn.gelu(pre).astype(jnp.bfloat16)
        outputs = jnp.dot(hidden, w_out, preferred_element_type=jnp.float32) + b_out
        return outputs.T.astype(jnp.bfloat16)
    values = lax.map(forward, blocks).reshape(n_samp, n_mem, n_vars, n_pts)
    ens = values.astype(jnp.float32)
    epsil = (1.0 - ALPHA) / n_mem
    skill = lax.optimization_barrier(jnp.sum(jnp.abs(ens - targets[:, None]), axis=1))
    spread = jnp.zeros_like(skill)
    for first in range(n_mem):
        spread = spread + lax.optimization_barrier(jnp.sum(jnp.abs(ens[:, first:first + 1] - ens), axis=1))
    weight = area[None, :] * var_weight[:, None]
    cell = weight[None] * (skill / n_mem - (1.0 - epsil) / (2.0 * n_mem * (n_mem - 1)) * spread)
    loss = lax.optimization_barrier(jnp.sum(cell, axis=(1, 2))) / (n_pts * n_vars)
    sign = jnp.where(member_rank >= obs_rank[:, None], 1.0, -1.0).astype(jnp.float32)
    centred = (2 * member_rank - n_mem + 1).astype(jnp.float32)
    cotangent = (weight[None, None] * (sign - (1.0 - epsil) / (n_mem - 1) * centred)).astype(jnp.bfloat16)
    scale = 1.0 / math.sqrt(n_samp * n_mem * n_pts)

    def backward(carry, items):
        rows, back = items
        pre = jnp.dot(rows, w_in, preferred_element_type=jnp.float32) + b_in
        hidden = jax.nn.gelu(pre).astype(jnp.bfloat16)
        g_out = carry[1] + jnp.einsum('ph,vp->hv', hidden, back, preferred_element_type=jnp.float32)
        g_bout = carry[3] + lax.optimization_barrier(jnp.sum(back.astype(jnp.float32), axis=1))
        upward = jnp.einsum('vp,hv->ph', back, w_out, preferred_element_type=jnp.float32)
        pullback = jax.vjp(jax.nn.gelu, pre)[1]
        dhidden = pullback(upward)[0].astype(jnp.bfloat16)
        g_in = carry[0] + jnp.einsum('pl,ph->lh', rows, dhidden, preferred_element_type=jnp.float32)
        g_bin = carry[2] + lax.optimization_barrier(jnp.sum(dhidden.astype(jnp.float32), axis=0))
        return ((g_in, g_out, g_bin, g_bout), None)
    start = (jnp.zeros(w_in.shape, jnp.float32), jnp.zeros(w_out.shape, jnp.float32), jnp.zeros(b_in.shape, jnp.float32), jnp.zeros(b_out.shape, jnp.float32))
    final = lax.scan(backward, start, (blocks, cotangent.reshape(n_samp * n_mem, n_vars, n_pts)))[0]
    return (loss, final[0] * scale, final[1] * scale, final[2] * scale, final[3] * scale)
```

```python
import math

import jax
import jax.numpy as jnp
from jax import lax
from jax.sharding import Mesh
from jax.sharding import PartitionSpec as P

ALPHA = 0.95
NAMES = ("y", "zlo", "x", "core", "zhi")
PLANE = ("y", "zlo", "x")
GRID = ("zlo", "x", "core")


def shift(axis, step):
    size = lax.axis_size(axis)
    return [(i, (i + step) % size) for i in range(size)]


def exchange(blocks, axis):
    size = blocks.shape[0]
    me = lax.axis_index(axis)
    out = blocks
    for step in range(1, size):
        part = lax.dynamic_index_in_dim(blocks, (me + step) % size, 0, keepdims=False)
        got = lax.ppermute(part, axis, shift(axis, step))
        out = lax.dynamic_update_index_in_dim(out, got, (me - step) % size, 0)
    return out


def low_part(value):
    return value - lax.reduce_precision(value, 8, 7)


def pack(extra):
    return jnp.concatenate(
        [extra, low_part(extra[:, 100:]), jnp.zeros((extra.shape[0], 22), jnp.float32)], axis=1
    ).astype(jnp.bfloat16)


def unpack(packed):
    wide = packed.astype(jnp.float32)
    low = jnp.pad(wide[..., 103:106], [(0, 0)] * (wide.ndim - 1) + [(100, 0)])
    return wide[..., :103] + low


def per_device(latents, w_in, b_in, w_out, b_out, targets, area, var_weight, member_rank, obs_rank):
    mem_dev = latents.shape[1]
    pts_dev = latents.shape[2]
    width = latents.shape[3]
    hid = w_in.shape[1]
    n_vars = w_out.shape[1]
    n_y = lax.axis_size("y")
    n_mem = mem_dev * n_y
    sub = pts_dev // n_y
    n_points = pts_dev * lax.axis_size(GRID)
    core = lax.axis_index("core")
    zhi = lax.axis_index("zhi")
    epsil = (1.0 - ALPHA) / n_mem
    scale = 1.0 / math.sqrt(lax.axis_size("zhi") * n_mem * n_points)

    weight = area[None, :] * var_weight[:, None]
    ranks = member_rank[0]
    sign = jnp.where(ranks >= obs_rank[0][None], 1.0, -1.0).astype(jnp.float32)
    centred = (2 * ranks - n_mem + 1).astype(jnp.float32)
    cot = (weight[None] * (sign - (1.0 - epsil) / (n_mem - 1) * centred)).astype(jnp.bfloat16)
    part_bout = jnp.sum(cot.astype(jnp.float32), axis=(0, 2))
    back = exchange(cot.reshape(n_y, mem_dev, n_vars, sub), "y")
    back = back.transpose(1, 2, 0, 3).reshape(mem_dev, n_vars, pts_dev)

    rows_x = latents.reshape(mem_dev * pts_dev, width)
    pre = jnp.dot(rows_x, w_in, preferred_element_type=jnp.float32) + b_in
    hidden = jax.nn.gelu(pre).astype(jnp.bfloat16)
    hidden3 = hidden.reshape(mem_dev, pts_dev, hid)
    values = (
        jnp.einsum("mph,hv->mvp", hidden3, w_out, preferred_element_type=jnp.float32)
        + b_out[None, :, None]
    ).astype(jnp.bfloat16)
    sent = values.reshape(mem_dev, n_vars, n_y, sub).transpose(2, 0, 1, 3)
    ens = exchange(sent, "y").reshape(n_mem, n_vars, sub).astype(jnp.float32)
    skill = jnp.sum(jnp.abs(ens - targets[0][None]), axis=0)
    spread = jnp.zeros_like(skill)
    for first in range(n_mem):
        spread = spread + jnp.sum(jnp.abs(ens[first : first + 1] - ens), axis=0)
    part_loss = jnp.sum(
        weight * (skill / n_mem - (1.0 - epsil) / (2.0 * n_mem * (n_mem - 1)) * spread)
    )

    upward = jnp.einsum("mvp,hv->mph", back, w_out, preferred_element_type=jnp.float32)
    pullback = jax.vjp(jax.nn.gelu, pre)[1]
    dhidden = pullback(upward.reshape(mem_dev * pts_dev, hid))[0].astype(jnp.bfloat16)
    part_out = jnp.einsum("mph,mvp->hv", hidden3, back, preferred_element_type=jnp.float32)
    part_bin = jnp.sum(dhidden.astype(jnp.float32), axis=0)
    part_in = jnp.einsum("rl,rh->lh", rows_x, dhidden, preferred_element_type=jnp.float32)

    extra = jnp.concatenate(
        [
            part_out,
            part_bin[:, None],
            jnp.pad(part_bout, (0, hid - n_vars))[:, None],
            jnp.where(jnp.arange(hid) == zhi, part_loss, 0.0)[:, None],
        ],
        axis=1,
    )

    n_plane = lax.axis_size(PLANE)
    block = width // (2 * n_plane)
    in4 = part_in.reshape(n_plane, 2, block, hid)
    ex4 = extra.reshape(n_plane, 2, block, 103)
    other = [(0, 1), (1, 0)]
    pick = lambda arr, which: lax.dynamic_index_in_dim(arr, which, 1, keepdims=False)
    got_in = lax.ppermute(pick(in4, 1 - core).astype(jnp.bfloat16), "core", other)
    got_ex = lax.ppermute(pick(ex4, 1 - core), "core", other)
    half_in = pick(in4, core) + got_in.astype(jnp.float32)
    half_ex = pick(ex4, core) + got_ex

    packed = pack(half_ex.reshape(n_plane * block, 103)).reshape(n_plane, block, 128)
    payload = jnp.concatenate([half_in.astype(jnp.bfloat16), packed], axis=2)
    landed = lax.all_to_all(payload, PLANE, 0, 0, tiled=True)
    sum_in = jnp.sum(landed[..., :hid].astype(jnp.float32), axis=0)
    sum_ex = jnp.sum(unpack(landed[..., hid:]), axis=0)

    n_zhi = lax.axis_size("zhi")
    rows4 = sum_in.reshape(n_zhi, block // n_zhi, hid)
    sum_ex = jnp.pad(sum_ex, ((0, 0), (0, 25)))
    total_in = lax.dynamic_index_in_dim(rows4, zhi, 0, keepdims=False)
    from_zhi = jnp.broadcast_to(sum_ex[None], (n_zhi, block, 128))
    for step in range(1, n_zhi):
        part = lax.dynamic_index_in_dim(rows4, (zhi + step) % n_zhi, 0, keepdims=False)
        both = jnp.concatenate([part.reshape(-1, 128), sum_ex], axis=0)
        got = lax.ppermute(both, "zhi", shift("zhi", step))
        total_in = total_in + got[: -block].reshape(block // n_zhi, hid)
        source = (zhi - step) % n_zhi
        from_zhi = lax.dynamic_update_index_in_dim(from_zhi, got[-block:], source, 0)
    total_ex = jnp.sum(from_zhi, axis=0)

    copies = jnp.broadcast_to(total_ex[None], (n_plane, block, 128))
    mine = lax.all_to_all(copies, PLANE, 0, 0, tiled=True)
    theirs = lax.ppermute(mine, "core", other)
    first = jnp.where(core == 0, mine, theirs)
    second = jnp.where(core == 0, theirs, mine)
    full = jnp.stack([first, second], axis=1).reshape(hid, 128)
    grad_out = full[:, :n_vars] * scale
    grad_bin = full[:, n_vars] * scale
    grad_bout = full[:n_vars, n_vars + 1] * scale
    loss = lax.dynamic_slice(full[:, n_vars + 2], (zhi,), (1,)) / (n_points * n_vars)
    return (loss, total_in * scale, grad_out, grad_bin, grad_bout)


def solution(mesh):
    split = Mesh(mesh.devices.reshape(4, 2, 4, 2, 4), NAMES)
    points = GRID + ("y",)
    in_specs = (
        P("zhi", "y", GRID, None),
        P(),
        P(),
        P(),
        P(),
        P("zhi", None, points),
        P(points),
        P(),
        P("zhi", None, None, points),
        P("zhi", None, points),
    )
    out_specs = (P("zhi"), P(NAMES, None), P(), P(), P())
    return jax.shard_map(
        per_device, mesh=split, in_specs=in_specs, out_specs=out_specs, check_vma=False
    )
```

```python
import math

import jax
import jax.numpy as jnp
from jax import lax
from jax.experimental import pallas as pl
from jax.experimental.pallas import tpu as pltpu
from jax.sharding import Mesh
from jax.sharding import PartitionSpec as P

ALPHA = 0.95
NAMES = ("y", "zlo", "x", "core", "zhi")
PLANE = ("y", "zlo", "x")
GRID = ("zlo", "x", "core")
F32 = jnp.float32
BF16 = jnp.bfloat16
GELU_C = math.sqrt(2.0 / math.pi)
GELU_A = 0.044715
LARGE = pltpu.CompilerParams(vmem_limit_bytes=60 * 1024 * 1024)
SMALL = pltpu.CompilerParams(vmem_limit_bytes=24 * 1024 * 1024)
SMEM = pl.BlockSpec(memory_space=pltpu.SMEM)

PER_BLOCK = 13
ROW_BIN, ROW_BOUT, ROW_LOSS = 121, 122, 15


def shift(axis, step):
    size = lax.axis_size(axis)
    return [(i, (i + step) % size) for i in range(size)]


def const_spec(shape):
    return pl.BlockSpec(shape, lambda *_: (0,) * len(shape))


def fold(block):
    row = lax.broadcasted_iota(jnp.int32, block.shape, 0)
    up = pltpu.roll(block, 12, 0)
    low = (row == 13) | (row == 14)
    return jnp.where((row == 9) | (row == 10), block + up, jnp.where(low, 0.0, block))


def unfold(block):
    row = lax.broadcasted_iota(jnp.int32, block.shape, 0)
    low = block - block.astype(BF16).astype(F32)
    return jnp.where((row == 13) | (row == 14), pltpu.roll(low, 4, 0), block)


def cotangent_kernel(
    ids, rank_ref, obs_ref, area_ref, vw_ref, weight_ref, bout_ref, send0, send1, send2, send3, every
):
    n_mem, sub, n_vars = rank_ref.shape
    mem_dev = n_mem // 4
    epsil = (1.0 - ALPHA) / n_mem
    row = lax.broadcasted_iota(jnp.int32, (sub, sub), 0)
    lane = lax.broadcasted_iota(jnp.int32, (sub, sub), 1)
    area = jnp.sum(jnp.where(row == lane, area_ref[...], 0.0), axis=1, keepdims=True)
    weight = area * vw_ref[...]
    weight_ref[...] = weight
    obs = obs_ref[...]
    total = jnp.zeros_like(weight)
    for member in range(n_mem):
        rank = rank_ref[member]
        sign = jnp.where(rank >= obs, 1.0, -1.0)
        centred = (2 * rank - n_mem + 1).astype(F32)
        cot = (weight * (sign - (1.0 - epsil) / (n_mem - 1) * centred)).astype(BF16)
        every[member // mem_dev, member % mem_dev] = cot
        total = total + cot.astype(F32)
    bout_ref[...] = jnp.sum(total, axis=0, keepdims=True)
    y = ids[0]
    for k, out in enumerate((send0, send1, send2, send3)):
        out[...] = every[lax.rem(y + k, 4)]


def forward_kernel(
    ids, x_ref, w_in_ref, b_in_ref, w_out_ref, b_out_ref,
    hidden_ref, slope_ref, send0, send1, send2, send3, every,
):
    step = pl.program_id(0)
    n_vars, hid = w_out_ref.shape
    sub = x_ref.shape[0] // 4
    x = x_ref[...]
    values = b_out_ref[...]
    for start in range(0, hid, 512):
        cols = slice(start, start + 512)
        pre = jnp.dot(x, w_in_ref[:, cols], preferred_element_type=F32) + b_in_ref[:, cols]
        square = pre * pre
        t = jnp.tanh(pre * (GELU_C + (GELU_C * GELU_A) * square))
        half = 0.5 + 0.5 * t
        hidden = (pre * half).astype(BF16)
        hidden_ref[:, cols] = hidden
        slope_ref[:, cols] = half + pre * (0.5 - 0.5 * (t * t)) * (
            GELU_C + (3.0 * GELU_A * GELU_C) * square
        )
        values = values + lax.dot_general(
            hidden, w_out_ref[:, cols], (((1,), (1,)), ((), ())), preferred_element_type=F32
        )
    values = values.astype(BF16).reshape(4, sub, n_vars)
    for dest in range(4):
        every[dest, step] = values[dest]

    @pl.when(step == 3)
    def _():
        y = ids[0]
        for k, out in enumerate((send0, send1, send2, send3)):
            out[...] = every[lax.rem(y + k, 4)]


def loss_kernel(got0, got1, got2, got3, target_ref, weight_ref, loss_ref):
    gots = (got0, got1, got2, got3)
    mem_dev = got0.shape[0]
    n_mem = 4 * mem_dev
    epsil = (1.0 - ALPHA) / n_mem
    ens = [got[m].astype(F32) for got in gots for m in range(mem_dev)]
    truth = target_ref[...]
    skill = jnp.zeros_like(truth)
    spread = jnp.zeros_like(truth)
    for j in range(n_mem):
        skill = skill + jnp.abs(ens[j] - truth)
        for k in range(j):
            spread = spread + jnp.abs(ens[j] - ens[k])
    cell = weight_ref[...] * (skill / n_mem - (1.0 - epsil) / (n_mem * (n_mem - 1)) * spread)
    loss_ref[...] = jnp.zeros((8, 128), F32) + jnp.sum(cell)


def backward_kernel(
    ids, got0, got1, got2, got3, x_ref, hidden_ref, slope_ref, w_out_ref, bout_ref,
    keep_ref, send_ref, keep_small, send_small, back, back_wide, small,
):
    step = pl.program_id(0)
    last = pl.num_programs(0) - 1
    mem_dev, sub, n_vars = got0.shape
    core = ids[2]
    cols = hidden_ref.shape[1]

    @pl.when(step == 0)
    def _():
        y = ids[0]
        for k, got in enumerate((got0, got1, got2, got3)):
            source = lax.rem(y + 4 - k, 4)
            for m in range(mem_dev):
                start = pl.multiple_of(m * 4 * sub + source * sub, sub)
                back[pl.ds(start, sub), :] = got[m]
        var = lax.broadcasted_iota(jnp.int32, (n_vars, 128), 0)
        lane = lax.broadcasted_iota(jnp.int32, (n_vars, 128), 1)
        place = jnp.where(lane == var + 3 * (var // PER_BLOCK), 1.0, 0.0).astype(BF16)
        back_wide[...] = jnp.dot(back[...], place, preferred_element_type=F32).astype(BF16)

    col = pl.multiple_of(step * cols, cols)
    upward = jnp.dot(back[...], w_out_ref[...], preferred_element_type=F32)
    dhidden = (upward * slope_ref[...]).astype(BF16)
    small[:, pl.ds(col, cols)] = lax.dot_general(
        back_wide[...], hidden_ref[...], (((0,), (0,)), ((), ())), preferred_element_type=F32
    )
    small[ROW_BIN : ROW_BIN + 1, pl.ds(col, cols)] = jnp.sum(
        dhidden.astype(F32), axis=0, keepdims=True
    )
    grad = lax.dot_general(
        x_ref[...], dhidden, (((0,), (0,)), ((), ())), preferred_element_type=F32
    )
    grad = grad.reshape(32, 2, 16, cols)
    first, second = grad[:, 0], grad[:, 1]
    keep_ref[...] = jnp.where(core == 0, first, second)
    send_ref[...] = jnp.where(core == 0, second, first).astype(BF16)

    @pl.when(step == last)
    def _():
        small[ROW_BOUT : ROW_BOUT + 1, 0:n_vars] = bout_ref[...]
        for part in range(4):
            start = pl.multiple_of((2 * part + core) * 16, 16)
            rows = small[pl.ds(start, 16), :]
            for j in range(8):
                keep_small[part * 8 + j] = rows[:, j * 128 : (j + 1) * 128]
            start = pl.multiple_of((2 * part + 1 - core) * 16, 16)
            rows = unfold(small[pl.ds(start, 16), :]).astype(BF16)
            for j in range(8):
                send_small[part * 8 + j] = rows[:, j * 128 : (j + 1) * 128]


def payload_kernel(keep_ref, got_ref, keep_small, got_small, out_ref):
    hid = keep_ref.shape[2]
    out_ref[:, :, 0:hid] = (keep_ref[...] + got_ref[...].astype(F32)).astype(BF16)
    for j in range(keep_small.shape[0]):
        block = unfold(keep_small[j] + fold(got_small[j].astype(F32)))
        out_ref[j, :, hid:] = block.astype(BF16)


def plane_kernel(ids, landed_ref, own_ref, small_ref, part1, part2, part3):
    hid = own_ref.shape[1]
    total = jnp.sum(landed_ref[...].astype(F32), axis=0)
    small = fold(total[:, hid:])
    small_ref[...] = small
    zhi = ids[1]
    quarters = [total[4 * z : 4 * z + 4, 0:hid] for z in range(4)]

    def quarter(which):
        out = quarters[3]
        for z in range(3):
            out = jnp.where(which == z, quarters[z], out)
        return out

    own_ref[...] = quarter(zhi)
    for k, out in ((1, part1), (2, part2), (3, part3)):
        rows = quarter(lax.rem(zhi + k, 4))
        for j in range(4):
            out[4 * j : 4 * j + 4, 0:256] = rows[:, j * 256 : (j + 1) * 256]
        out[:, 256:384] = small


def total_kernel(scale, ids, own_ref, small_ref, got1, got2, got3, loss_ref, grad_ref, copies_ref):
    zhi = ids[1]
    for j in range(4):
        acc = own_ref[:, j * 256 : (j + 1) * 256]
        for got in (got1, got2, got3):
            acc = acc + got[4 * j : 4 * j + 4, 0:256]
        grad_ref[:, j * 256 : (j + 1) * 256] = acc * scale
    parts = [small_ref[...]] + [got[:, 256:384] for got in (got1, got2, got3)]
    acc = None
    for source in range(4):
        term = parts[0]
        for k in range(1, 4):
            term = jnp.where(lax.rem(zhi + 4 - k, 4) == source, parts[k], term)
        acc = term if acc is None else acc + term
    row = lax.broadcasted_iota(jnp.int32, acc.shape, 0)
    acc = jnp.where(row == ROW_LOSS, loss_ref[0:1, :], acc)
    copies_ref[...] = jnp.broadcast_to(acc[None], copies_ref.shape)


def final_kernel(scale, loss_scale, ids, mine, theirs, out_ref, bin_ref, bout_ref, loss_ref, full):
    core = ids[2]
    n_vars = out_ref.shape[0]
    for which, blocks in ((core, mine), (1 - core, theirs)):
        for part in range(4):
            start = pl.multiple_of((2 * part + which) * 16, 16)
            for j in range(8):
                full[pl.ds(start, 16), j * 128 : (j + 1) * 128] = blocks[part * 8 + j]
    for q in range(8):
        count = min(PER_BLOCK, n_vars - PER_BLOCK * q)
        out_ref[PER_BLOCK * q : PER_BLOCK * q + count, :] = full[16 * q : 16 * q + count, :] * scale
    bin_ref[...] = full[ROW_BIN : ROW_BIN + 1, :] * scale
    bout_ref[...] = full[ROW_BOUT : ROW_BOUT + 1, 0:n_vars] * scale
    total = jnp.zeros((1, 128), F32)
    for q in range(8):
        for j in range(8):
            total = total + full[16 * q + ROW_LOSS : 16 * q + ROW_LOSS + 1, 128 * j : 128 * (j + 1)]
    loss_ref[...] = total[:, 0:1] * loss_scale


def per_device(latents, w_in, b_in, w_out, b_out, targets, area, var_weight, member_rank, obs_rank):
    mem_dev = latents.shape[1]
    pts_dev = latents.shape[2]
    width = latents.shape[3]
    hid = w_in.shape[1]
    n_vars = w_out.shape[1]
    n_y = lax.axis_size("y")
    n_mem = mem_dev * n_y
    sub = pts_dev // n_y
    rows = mem_dev * pts_dev
    n_points = pts_dev * lax.axis_size(GRID)
    scale = 1.0 / math.sqrt(lax.axis_size("zhi") * n_mem * n_points)
    ids = jnp.stack(
        [lax.axis_index("y"), lax.axis_index("zhi"), lax.axis_index("core")]
    ).astype(jnp.int32)
    shape = jax.ShapeDtypeStruct

    x = latents.reshape(rows, width)
    w_out_t = w_out.T
    ranks = member_rank[0].transpose(0, 2, 1)
    obs = obs_rank[0].T
    truth = targets[0].T
    sent = shape((mem_dev, sub, n_vars), BF16)
    whole = pl.BlockSpec(memory_space=pltpu.VMEM)

    weight, bout, cot0, cot1, cot2, cot3 = pl.pallas_call(
        cotangent_kernel,
        in_specs=[SMEM] + [whole] * 4,
        out_shape=[shape((sub, n_vars), F32), shape((1, n_vars), F32)] + [sent] * 4,
        scratch_shapes=[pltpu.VMEM((n_y, mem_dev, sub, n_vars), BF16)],
        compiler_params=SMALL,
        name="cotangent",
    )(ids, ranks, obs, area[None, :], var_weight[None, :])
    ids_later, cot1, cot2, cot3 = lax.optimization_barrier((ids, cot1, cot2, cot3))
    cot1 = lax.ppermute(cot1, "y", shift("y", 1))
    cot2 = lax.ppermute(cot2, "y", shift("y", 2))
    cot3 = lax.ppermute(cot3, "y", shift("y", 3))

    hidden, slope, val0, val1, val2, val3 = pl.pallas_call(
        forward_kernel,
        grid=(mem_dev,),
        in_specs=[
            SMEM,
            pl.BlockSpec((pts_dev, width), lambda i: (i, 0)),
            const_spec((width, hid)),
            const_spec((1, hid)),
            const_spec((n_vars, hid)),
            const_spec((1, n_vars)),
        ],
        out_specs=[
            pl.BlockSpec((pts_dev, hid), lambda i: (i, 0)),
            pl.BlockSpec((pts_dev, hid), lambda i: (i, 0)),
        ]
        + [const_spec(sent.shape)] * 4,
        out_shape=[shape((rows, hid), BF16), shape((rows, hid), F32)] + [sent] * 4,
        scratch_shapes=[pltpu.VMEM((n_y, mem_dev, sub, n_vars), BF16)],
        compiler_params=LARGE,
        name="forward",
    )(ids_later, x, w_in, b_in[None, :], w_out_t, b_out[None, :])

    cols = 512
    n_plane = lax.axis_size(PLANE)
    block = width // (2 * n_plane)
    keep, send, keep_small, send_small = pl.pallas_call(
        backward_kernel,
        grid=(hid // cols,),
        in_specs=[SMEM]
        + [const_spec(sent.shape)] * 4
        + [
            const_spec((rows, width)),
            pl.BlockSpec((rows, cols), lambda i: (0, i)),
            pl.BlockSpec((rows, cols), lambda i: (0, i)),
            pl.BlockSpec((n_vars, cols), lambda i: (0, i)),
            const_spec((1, n_vars)),
        ],
        out_specs=[
            pl.BlockSpec((n_plane, block, cols), lambda i: (0, 0, i)),
            pl.BlockSpec((n_plane, block, cols), lambda i: (0, 0, i)),
            const_spec((n_plane, block, 128)),
            const_spec((n_plane, block, 128)),
        ],
        out_shape=[
            shape((n_plane, block, hid), F32),
            shape((n_plane, block, hid), BF16),
            shape((n_plane, block, 128), F32),
            shape((n_plane, block, 128), BF16),
        ],
        scratch_shapes=[
            pltpu.VMEM((rows, n_vars), BF16),
            pltpu.VMEM((rows, 128), BF16),
            pltpu.VMEM((128, hid), F32),
        ],
        compiler_params=LARGE,
        name="backward",
    )(ids, cot0, cot1, cot2, cot3, x, hidden, slope, w_out_t, bout)

    swap = [(0, 1), (1, 0)]
    got = lax.ppermute(send, "core", swap)
    got_small = lax.ppermute(send_small, "core", swap)
    payload = pl.pallas_call(
        payload_kernel,
        out_shape=shape((n_plane, block, hid + 128), BF16),
        compiler_params=SMALL,
        name="payload",
    )(keep, got, keep_small, got_small)
    payload, val1, val2, val3 = lax.optimization_barrier((payload, val1, val2, val3))
    landed = lax.all_to_all(payload, PLANE, 0, 0, tiled=True)
    val1 = lax.ppermute(val1, "y", shift("y", 1))
    val2 = lax.ppermute(val2, "y", shift("y", 2))
    val3 = lax.ppermute(val3, "y", shift("y", 3))
    part_loss = pl.pallas_call(
        loss_kernel, out_shape=shape((8, 128), F32), compiler_params=SMALL, name="loss"
    )(val0, val1, val2, val3, truth, weight)

    part = shape((block, 384), F32)
    own, small, part1, part2, part3 = pl.pallas_call(
        plane_kernel,
        in_specs=[SMEM, whole],
        out_shape=[shape((block // 4, hid), F32), shape((block, 128), F32), part, part, part],
        compiler_params=SMALL,
        name="plane_sum",
    )(ids, landed)
    part1 = lax.ppermute(part1, "zhi", shift("zhi", 1))
    part2 = lax.ppermute(part2, "zhi", shift("zhi", 2))
    part3 = lax.ppermute(part3, "zhi", shift("zhi", 3))
    grad_in, copies = pl.pallas_call(
        lambda *refs: total_kernel(scale, *refs),
        in_specs=[SMEM] + [whole] * 6,
        out_shape=[shape((block // 4, hid), F32), shape((n_plane, block, 128), F32)],
        compiler_params=SMALL,
        name="total",
    )(ids, own, small, part1, part2, part3, part_loss)

    mine = lax.all_to_all(copies, PLANE, 0, 0, tiled=True)
    theirs = lax.ppermute(mine, "core", swap)
    grad_out, grad_bin, grad_bout, loss = pl.pallas_call(
        lambda *refs: final_kernel(scale, 1.0 / (n_points * n_vars), *refs),
        in_specs=[SMEM] + [whole] * 2,
        out_shape=[
            shape((n_vars, hid), F32),
            shape((1, hid), F32),
            shape((1, n_vars), F32),
            shape((1, 1), F32),
        ],
        scratch_shapes=[pltpu.VMEM((128, hid), F32)],
        compiler_params=SMALL,
        name="unpack",
    )(ids, mine, theirs)
    return (loss.reshape(1), grad_in, grad_out.T, grad_bin.reshape(hid), grad_bout.reshape(n_vars))


def solution(mesh):
    split = Mesh(mesh.devices.reshape(4, 2, 4, 2, 4), NAMES)
    points = GRID + ("y",)
    in_specs = (
        P("zhi", "y", GRID, None),
        P(),
        P(),
        P(),
        P(),
        P("zhi", None, points),
        P(points),
        P(),
        P("zhi", None, None, points),
        P("zhi", None, points),
    )
    out_specs = (P("zhi"), P(NAMES, None), P(), P(), P())
    return jax.shard_map(
        per_device, mesh=split, in_specs=in_specs, out_specs=out_specs, check_vma=False
    )
```

```python
import math

import jax
import jax.numpy as jnp
from jax import lax
from jax.experimental import pallas as pl
from jax.experimental.pallas import tpu as pltpu
from jax.sharding import Mesh
from jax.sharding import PartitionSpec as P

ALPHA = 0.95
NAMES = ("y", "zlo", "x", "core", "zhi")
PLANE = ("y", "zlo", "x")
GRID = ("zlo", "x", "core")
F32 = jnp.float32
BF16 = jnp.bfloat16
GELU_C = math.sqrt(2.0 / math.pi)
GELU_A = 0.044715
PARAMS = pltpu.CompilerParams(vmem_limit_bytes=24 * 1024 * 1024)
SMEM = pl.BlockSpec(memory_space=pltpu.SMEM)

PER_BLOCK = 13
ROW_BIN, ROW_BOUT, ROW_LOSS = 121, 122, 15


def shift(axis, step):
    size = lax.axis_size(axis)
    return [(i, (i + step) % size) for i in range(size)]


def const_spec(shape):
    return pl.BlockSpec(shape, lambda *_: (0,) * len(shape))


def fold(block):
    row = lax.broadcasted_iota(jnp.int32, block.shape, 0)
    up = pltpu.roll(block, 12, 0)
    low = (row == 13) | (row == 14)
    return jnp.where((row == 9) | (row == 10), block + up, jnp.where(low, 0.0, block))


def unfold(block):
    row = lax.broadcasted_iota(jnp.int32, block.shape, 0)
    low = block - block.astype(BF16).astype(F32)
    return jnp.where((row == 13) | (row == 14), pltpu.roll(low, 4, 0), block)


def cotangent_kernel(
    ids, rank_hbm, obs_hbm, area_hbm, vw_hbm, x_hbm, w_in_hbm, b_in_hbm, w_out_hbm, b_out_hbm,
    weight_ref, bout_ref, send0, send1, send2, send3, x_ref, w_in_ref, b_in_ref, w_out_ref, b_out_ref,
    every, rank_ref, obs_ref, area_ref, vw_ref, sems,
):
    pairs = [(rank_hbm, rank_ref), (obs_hbm, obs_ref), (area_hbm, area_ref), (vw_hbm, vw_ref)]
    needed = len(pairs)
    pairs += [(w_out_hbm, w_out_ref), (b_in_hbm, b_in_ref), (b_out_hbm, b_out_ref)]
    for source, target in ((x_hbm, x_ref), (w_in_hbm, w_in_ref)):
        piece = source.shape[0] // 4
        for i in range(4):
            rows = pl.ds(i * piece, piece)
            pairs.append((source.at[rows, :], target.at[rows, :]))
    fetches = [
        pltpu.make_async_copy(source, target, sems.at[i]) for i, (source, target) in enumerate(pairs)
    ]
    for fetch in fetches:
        fetch.start()
    for fetch in fetches[:needed]:
        fetch.wait()
    n_mem, sub, n_vars = rank_ref.shape
    mem_dev = n_mem // 4
    epsil = (1.0 - ALPHA) / n_mem
    row = lax.broadcasted_iota(jnp.int32, (sub, sub), 0)
    lane = lax.broadcasted_iota(jnp.int32, (sub, sub), 1)
    area = jnp.sum(jnp.where(row == lane, area_ref[...], 0.0), axis=1, keepdims=True)
    weight = area * vw_ref[...]
    weight_ref[...] = weight
    obs = obs_ref[...]
    total = jnp.zeros_like(weight)
    for member in range(n_mem):
        rank = rank_ref[member]
        sign = jnp.where(rank >= obs, 1.0, -1.0)
        centred = (2 * rank - n_mem + 1).astype(F32)
        cot = (weight * (sign - (1.0 - epsil) / (n_mem - 1) * centred)).astype(BF16)
        every[member // mem_dev, member % mem_dev] = cot
        total = total + cot.astype(F32)
    bout_ref[...] = jnp.sum(total, axis=0, keepdims=True)
    y = ids[0]
    for k, out in enumerate((send0, send1, send2, send3)):
        out[...] = every[lax.rem(y + k, 4)]
    for fetch in fetches[needed:]:
        fetch.wait()


def forward_kernel(
    ids, x_ref, w_in_ref, b_in_ref, w_out_ref, b_out_ref,
    hidden_ref, slope_ref, send0, send1, send2, send3, values,
):
    step = pl.program_id(0)
    mem_dev, sub, _ = send0.shape
    pre = jnp.dot(x_ref[...], w_in_ref[...], preferred_element_type=F32) + b_in_ref[...]
    square = pre * pre
    t = jnp.tanh(pre * (GELU_C + (GELU_C * GELU_A) * square))
    half = 0.5 + 0.5 * t
    hidden = (pre * half).astype(BF16)
    hidden_ref[...] = hidden
    slope_ref[...] = half + pre * (0.5 - 0.5 * (t * t)) * (
        GELU_C + (3.0 * GELU_A * GELU_C) * square
    )
    part = lax.dot_general(
        hidden, w_out_ref[...], (((1,), (1,)), ((), ())), preferred_element_type=F32
    )

    @pl.when(step == 0)
    def _():
        values[...] = part + b_out_ref[...]

    @pl.when(step > 0)
    def _():
        values[...] += part

    @pl.when(step == pl.num_programs(0) - 1)
    def _():
        y = ids[0]
        for k, out in enumerate((send0, send1, send2, send3)):
            dest = lax.rem(y + k, 4)
            for m in range(mem_dev):
                start = pl.multiple_of(m * 4 * sub + dest * sub, sub)
                out[m] = values[pl.ds(start, sub), :].astype(BF16)


def loss_kernel(got0, got1, got2, got3, target_ref, weight_ref, loss_ref):
    gots = (got0, got1, got2, got3)
    mem_dev = got0.shape[0]
    n_mem = 4 * mem_dev
    epsil = (1.0 - ALPHA) / n_mem
    ens = [got[m].astype(F32) for got in gots for m in range(mem_dev)]
    truth = target_ref[...]
    skill = jnp.zeros_like(truth)
    spread = jnp.zeros_like(truth)
    for j in range(n_mem):
        skill = skill + jnp.abs(ens[j] - truth)
        for k in range(j):
            spread = spread + jnp.abs(ens[j] - ens[k])
    cell = weight_ref[...] * (skill / n_mem - (1.0 - epsil) / (n_mem * (n_mem - 1)) * spread)
    loss_ref[...] = jnp.zeros((8, 128), F32) + jnp.sum(cell)


def backward_kernel(
    ids, got0, got1, got2, got3, x_ref, hidden_ref, slope_ref, w_out_ref, bout_ref,
    keep_ref, send_ref, back, back_wide, small,
):
    mem_dev, sub, n_vars = got0.shape
    core = ids[2]
    hid = hidden_ref.shape[1]
    y = ids[0]
    for k, got in enumerate((got0, got1, got2, got3)):
        source = lax.rem(y + 4 - k, 4)
        for m in range(mem_dev):
            start = pl.multiple_of(m * 4 * sub + source * sub, sub)
            back[pl.ds(start, sub), :] = got[m]
    var = lax.broadcasted_iota(jnp.int32, (n_vars, 128), 0)
    lane = lax.broadcasted_iota(jnp.int32, (n_vars, 128), 1)
    place = jnp.where(lane == var + 3 * (var // PER_BLOCK), 1.0, 0.0).astype(BF16)
    back_wide[...] = jnp.dot(back[...], place, preferred_element_type=F32).astype(BF16)

    for start in range(0, hid, 256):
        cols = slice(start, start + 256)
        upward = jnp.dot(back[...], w_out_ref[:, cols], preferred_element_type=F32)
        dhidden = (upward * slope_ref[:, cols]).astype(BF16)
        small[:, cols] = lax.dot_general(
            back_wide[...], hidden_ref[:, cols], (((0,), (0,)), ((), ())), preferred_element_type=F32
        )
        small[ROW_BIN : ROW_BIN + 1, cols] = jnp.sum(dhidden.astype(F32), axis=0, keepdims=True)
        grad = lax.dot_general(
            x_ref[...], dhidden, (((0,), (0,)), ((), ())), preferred_element_type=F32
        )
        grad = grad.reshape(32, 2, 16, 256)
        first, second = grad[:, 0], grad[:, 1]
        keep_ref[:, :, cols] = jnp.where(core == 0, first, second)
        send_ref[:, :, cols] = jnp.where(core == 0, second, first).astype(BF16)

    small[ROW_BOUT : ROW_BOUT + 1, 0:n_vars] = bout_ref[...]
    for part in range(4):
        start = pl.multiple_of((2 * part + core) * 16, 16)
        rows = small[pl.ds(start, 16), :]
        for j in range(8):
            keep_ref[part * 8 + j, :, hid:] = rows[:, j * 128 : (j + 1) * 128]
        start = pl.multiple_of((2 * part + 1 - core) * 16, 16)
        rows = unfold(small[pl.ds(start, 16), :]).astype(BF16)
        for j in range(8):
            send_ref[part * 8 + j, :, hid:] = rows[:, j * 128 : (j + 1) * 128]


def payload_kernel(keep_ref, got_ref, out_hbm, out_ref, sems):
    n_plane, _, width = keep_ref.shape
    hid = width - 128
    piece = n_plane // 4
    stores = []
    for i in range(4):
        part = slice(i * piece, (i + 1) * piece)
        total = keep_ref[part, :, 0:hid] + got_ref[part, :, 0:hid].astype(F32)
        out_ref[part, :, 0:hid] = total.astype(BF16)
        for j in range(i * piece, (i + 1) * piece):
            block = unfold(keep_ref[j, :, hid:] + fold(got_ref[j, :, hid:].astype(F32)))
            out_ref[j, :, hid:] = block.astype(BF16)
        part = pl.ds(i * piece, piece)
        store = pltpu.make_async_copy(out_ref.at[part], out_hbm.at[part], sems.at[i])
        store.start()
        stores.append(store)
    for store in stores:
        store.wait()


def plane_kernel(ids, landed_ref, own_ref, small_ref, part1, part2, part3):
    hid = own_ref.shape[1]
    total = jnp.sum(landed_ref[...].astype(F32), axis=0)
    small = fold(total[:, hid:])
    small_ref[...] = small
    zhi = ids[1]
    quarters = [total[4 * z : 4 * z + 4, 0:hid] for z in range(4)]

    def quarter(which):
        out = quarters[3]
        for z in range(3):
            out = jnp.where(which == z, quarters[z], out)
        return out

    own_ref[...] = quarter(zhi)
    for k, out in ((1, part1), (2, part2), (3, part3)):
        rows = quarter(lax.rem(zhi + k, 4))
        for j in range(4):
            out[4 * j : 4 * j + 4, 0:256] = rows[:, j * 256 : (j + 1) * 256]
        out[:, 256:384] = small


def total_kernel(scale, ids, own_ref, small_ref, got1, got2, got3, loss_ref, grad_ref, copies_ref):
    zhi = ids[1]
    for j in range(4):
        acc = own_ref[:, j * 256 : (j + 1) * 256]
        for got in (got1, got2, got3):
            acc = acc + got[4 * j : 4 * j + 4, 0:256]
        grad_ref[:, j * 256 : (j + 1) * 256] = acc * scale
    parts = [small_ref[...]] + [got[:, 256:384] for got in (got1, got2, got3)]
    acc = None
    for source in range(4):
        term = parts[0]
        for k in range(1, 4):
            term = jnp.where(lax.rem(zhi + 4 - k, 4) == source, parts[k], term)
        acc = term if acc is None else acc + term
    row = lax.broadcasted_iota(jnp.int32, acc.shape, 0)
    acc = jnp.where(row == ROW_LOSS, loss_ref[0:1, :], acc)
    copies_ref[...] = jnp.broadcast_to(acc[None], copies_ref.shape)


def final_kernel(scale, loss_scale, ids, mine, theirs, out_ref, bin_ref, bout_ref, loss_ref, full):
    core = ids[2]
    n_vars = out_ref.shape[0]
    for which, blocks in ((core, mine), (1 - core, theirs)):
        for part in range(4):
            start = pl.multiple_of((2 * part + which) * 16, 16)
            for j in range(8):
                full[pl.ds(start, 16), j * 128 : (j + 1) * 128] = blocks[part * 8 + j]
    for q in range(8):
        count = min(PER_BLOCK, n_vars - PER_BLOCK * q)
        out_ref[PER_BLOCK * q : PER_BLOCK * q + count, :] = full[16 * q : 16 * q + count, :] * scale
    bin_ref[...] = full[ROW_BIN : ROW_BIN + 1, :] * scale
    bout_ref[...] = full[ROW_BOUT : ROW_BOUT + 1, 0:n_vars] * scale
    total = jnp.zeros((1, 128), F32)
    for q in range(8):
        for j in range(8):
            total = total + full[16 * q + ROW_LOSS : 16 * q + ROW_LOSS + 1, 128 * j : 128 * (j + 1)]
    loss_ref[...] = total[:, 0:1] * loss_scale


def per_device(latents, w_in, b_in, w_out, b_out, targets, area, var_weight, member_rank, obs_rank):
    mem_dev = latents.shape[1]
    pts_dev = latents.shape[2]
    width = latents.shape[3]
    hid = w_in.shape[1]
    n_vars = w_out.shape[1]
    n_y = lax.axis_size("y")
    n_mem = mem_dev * n_y
    sub = pts_dev // n_y
    rows = mem_dev * pts_dev
    n_points = pts_dev * lax.axis_size(GRID)
    scale = 1.0 / math.sqrt(lax.axis_size("zhi") * n_mem * n_points)
    ids = jnp.stack(
        [lax.axis_index("y"), lax.axis_index("zhi"), lax.axis_index("core")]
    ).astype(jnp.int32)
    shape = jax.ShapeDtypeStruct

    x = latents.reshape(rows, width)
    w_out_t = w_out.T
    ranks = member_rank[0].transpose(0, 2, 1)
    obs = obs_rank[0].T
    truth = targets[0].T
    sent = shape((mem_dev, sub, n_vars), BF16)
    whole = pl.BlockSpec(memory_space=pltpu.VMEM)

    hbm = pl.BlockSpec(memory_space=pltpu.HBM)
    operands = [
        pltpu.with_memory_space_constraint(arr, pltpu.HBM)
        for arr in (
            ranks, obs, area[None, :], var_weight[None, :],
            x, w_in, b_in[None, :], w_out_t, b_out[None, :],
        )
    ]
    weight, bout, cot0, cot1, cot2, cot3, x, w_in, b_in, w_out_t, b_out = pl.pallas_call(
        cotangent_kernel,
        in_specs=[SMEM] + [hbm] * 9,
        out_specs=[whole] * 11,
        out_shape=[shape((sub, n_vars), F32), shape((1, n_vars), F32)]
        + [sent] * 4
        + [
            shape((rows, width), BF16),
            shape((width, hid), BF16),
            shape((1, hid), F32),
            shape((n_vars, hid), BF16),
            shape((1, n_vars), F32),
        ],
        scratch_shapes=[
            pltpu.VMEM((n_y, mem_dev, sub, n_vars), BF16),
            pltpu.VMEM((n_mem, sub, n_vars), jnp.int32),
            pltpu.VMEM((sub, n_vars), jnp.int32),
            pltpu.VMEM((1, sub), F32),
            pltpu.VMEM((1, n_vars), F32),
            pltpu.SemaphoreType.DMA((15,)),
        ],
        compiler_params=PARAMS,
        name="cotangent",
    )(ids, *operands)
    ids_later, cot1, cot2, cot3 = lax.optimization_barrier((ids, cot1, cot2, cot3))
    cot2 = lax.ppermute(cot2, "y", shift("y", 2))
    cot1 = lax.ppermute(cot1, "y", shift("y", 1))
    cot3 = lax.ppermute(cot3, "y", shift("y", 3))

    cols = 512
    by_cols = lambda height: pl.BlockSpec((height, cols), lambda i: (0, i))
    hidden, slope, val0, val1, val2, val3 = pl.pallas_call(
        forward_kernel,
        grid=(hid // cols,),
        in_specs=[
            SMEM,
            const_spec((rows, width)),
            by_cols(width),
            by_cols(1),
            by_cols(n_vars),
            const_spec((1, n_vars)),
        ],
        out_specs=[by_cols(rows), by_cols(rows)] + [const_spec(sent.shape)] * 4,
        out_shape=[shape((rows, hid), BF16), shape((rows, hid), F32)] + [sent] * 4,
        scratch_shapes=[pltpu.VMEM((rows, n_vars), F32)],
        compiler_params=PARAMS,
        name="forward",
    )(ids_later, x, w_in, b_in, w_out_t, b_out)

    n_plane = lax.axis_size(PLANE)
    block = width // (2 * n_plane)
    keep, send = pl.pallas_call(
        backward_kernel,
        in_specs=[SMEM] + [whole] * 9,
        out_specs=[whole] * 2,
        out_shape=[
            shape((n_plane, block, hid + 128), F32),
            shape((n_plane, block, hid + 128), BF16),
        ],
        scratch_shapes=[
            pltpu.VMEM((rows, n_vars), BF16),
            pltpu.VMEM((rows, 128), BF16),
            pltpu.VMEM((128, hid), F32),
        ],
        compiler_params=PARAMS,
        name="backward",
    )(ids, cot0, cot1, cot2, cot3, x, hidden, slope, w_out_t, bout)

    swap = [(0, 1), (1, 0)]
    got = lax.ppermute(send, "core", swap)
    payload_shape = (n_plane, block, hid + 128)
    payload = pl.pallas_call(
        payload_kernel,
        in_specs=[whole] * 2,
        out_specs=hbm,
        out_shape=shape(payload_shape, BF16),
        scratch_shapes=[pltpu.VMEM(payload_shape, BF16), pltpu.SemaphoreType.DMA((4,))],
        compiler_params=PARAMS,
        name="payload",
    )(keep, got)
    payload, val1, val2, val3 = lax.optimization_barrier((payload, val1, val2, val3))
    landed = lax.all_to_all(payload, PLANE, 0, 0, tiled=True)
    val2 = lax.ppermute(val2, "y", shift("y", 2))
    val1 = lax.ppermute(val1, "y", shift("y", 1))
    val3 = lax.ppermute(val3, "y", shift("y", 3))
    part_loss = pl.pallas_call(
        loss_kernel,
        in_specs=[whole] * 6,
        out_specs=whole,
        out_shape=shape((8, 128), F32),
        compiler_params=PARAMS,
        name="loss",
    )(val0, val1, val2, val3, truth, weight)

    part = shape((block, 384), F32)
    own, small, part1, part2, part3 = pl.pallas_call(
        plane_kernel,
        in_specs=[SMEM, whole],
        out_specs=[whole] * 5,
        out_shape=[shape((block // 4, hid), F32), shape((block, 128), F32), part, part, part],
        compiler_params=PARAMS,
        name="plane_sum",
    )(ids, landed)
    part2 = lax.ppermute(part2, "zhi", shift("zhi", 2))
    part1 = lax.ppermute(part1, "zhi", shift("zhi", 1))
    part3 = lax.ppermute(part3, "zhi", shift("zhi", 3))
    grad_in, copies = pl.pallas_call(
        lambda *refs: total_kernel(scale, *refs),
        in_specs=[SMEM] + [whole] * 6,
        out_specs=[whole] * 2,
        out_shape=[shape((block // 4, hid), F32), shape((n_plane, block, 128), F32)],
        compiler_params=PARAMS,
        name="total",
    )(ids, own, small, part1, part2, part3, part_loss)

    mine = lax.all_to_all(copies, PLANE, 0, 0, tiled=True)
    theirs = lax.ppermute(mine, "core", swap)
    grad_out, grad_bin, grad_bout, loss = pl.pallas_call(
        lambda *refs: final_kernel(scale, 1.0 / (n_points * n_vars), *refs),
        in_specs=[SMEM] + [whole] * 2,
        out_specs=[whole] * 4,
        out_shape=[
            shape((n_vars, hid), F32),
            shape((1, hid), F32),
            shape((1, n_vars), F32),
            shape((1, 1), F32),
        ],
        scratch_shapes=[pltpu.VMEM((128, hid), F32)],
        compiler_params=PARAMS,
        name="unpack",
    )(ids, mine, theirs)
    return (loss.reshape(1), grad_in, grad_out.T, grad_bin.reshape(hid), grad_bout.reshape(n_vars))


def solution(mesh):
    split = Mesh(mesh.devices.reshape(4, 2, 4, 2, 4), NAMES)
    points = GRID + ("y",)
    in_specs = (
        P("zhi", "y", GRID, None),
        P(),
        P(),
        P(),
        P(),
        P("zhi", None, points),
        P(points),
        P(),
        P("zhi", None, None, points),
        P("zhi", None, points),
    )
    out_specs = (P("zhi"), P(NAMES, None), P(), P(), P())
    return jax.shard_map(
        per_device, mesh=split, in_specs=in_specs, out_specs=out_specs, check_vma=False
    )
```

```python
import math

import jax
import jax.numpy as jnp
from jax import lax
from jax.experimental import pallas as pl
from jax.experimental.pallas import tpu as pltpu
from jax.sharding import Mesh
from jax.sharding import PartitionSpec as P

ALPHA = 0.95
NAMES = ("y", "zlo", "x", "core", "zhi")
PLANE = ("y", "zlo", "x")
GRID = ("zlo", "x", "core")
F32 = jnp.float32
BF16 = jnp.bfloat16
GELU_C = math.sqrt(2.0 / math.pi)
GELU_A = 0.044715
PARAMS = pltpu.CompilerParams(vmem_limit_bytes=24 * 1024 * 1024)
SMEM = pl.BlockSpec(memory_space=pltpu.SMEM)

PER_BLOCK = 13
ROW_BIN, ROW_BOUT, ROW_LOSS = 121, 122, 15


def shift(axis, step):
    size = lax.axis_size(axis)
    return [(i, (i + step) % size) for i in range(size)]


def pairs_of(axis, step):
    return [(i, i ^ step) for i in range(lax.axis_size(axis))]


def const_spec(shape):
    return pl.BlockSpec(shape, lambda *_: (0,) * len(shape))


def fold(block):
    row = lax.broadcasted_iota(jnp.int32, block.shape, 0)
    up = pltpu.roll(block, 12, 0)
    low = (row == 13) | (row == 14)
    return jnp.where((row == 9) | (row == 10), block + up, jnp.where(low, 0.0, block))


def unfold(block):
    row = lax.broadcasted_iota(jnp.int32, block.shape, 0)
    low = block - block.astype(BF16).astype(F32)
    return jnp.where((row == 13) | (row == 14), pltpu.roll(low, 4, 0), block)


def cotangent_kernel(
    ids, rank_hbm, obs_hbm, area_hbm, vw_hbm, x_hbm, w_in_hbm, b_in_hbm, w_out_hbm, b_out_hbm,
    weight_ref, bout_ref, send0, send2, send1, send3, x_ref, w_in_ref, b_in_ref, w_out_ref, b_out_ref,
    every, rank_ref, obs_ref, area_ref, vw_ref, sems,
):
    pairs = [(rank_hbm, rank_ref), (obs_hbm, obs_ref), (area_hbm, area_ref), (vw_hbm, vw_ref)]
    needed = len(pairs)
    pairs += [(w_out_hbm, w_out_ref), (b_in_hbm, b_in_ref), (b_out_hbm, b_out_ref)]
    for source, target in ((x_hbm, x_ref), (w_in_hbm, w_in_ref)):
        piece = source.shape[0] // 4
        for i in range(4):
            rows = pl.ds(i * piece, piece)
            pairs.append((source.at[rows, :], target.at[rows, :]))
    fetches = [
        pltpu.make_async_copy(source, target, sems.at[i]) for i, (source, target) in enumerate(pairs)
    ]
    for fetch in fetches:
        fetch.start()
    for fetch in fetches[:needed]:
        fetch.wait()
    n_mem, sub, n_vars = rank_ref.shape
    mem_dev = n_mem // 4
    epsil = (1.0 - ALPHA) / n_mem
    row = lax.broadcasted_iota(jnp.int32, (sub, sub), 0)
    lane = lax.broadcasted_iota(jnp.int32, (sub, sub), 1)
    area = jnp.sum(jnp.where(row == lane, area_ref[...], 0.0), axis=1, keepdims=True)
    weight = area * vw_ref[...]
    weight_ref[...] = weight
    obs = obs_ref[...]
    total = jnp.zeros_like(weight)
    for member in range(n_mem):
        rank = rank_ref[member]
        sign = jnp.where(rank >= obs, 1.0, -1.0)
        centred = (2 * rank - n_mem + 1).astype(F32)
        cot = (weight * (sign - (1.0 - epsil) / (n_mem - 1) * centred)).astype(BF16)
        every[member // mem_dev, member % mem_dev] = cot
        total = total + cot.astype(F32)
    bout_ref[...] = jnp.sum(total, axis=0, keepdims=True)
    y = ids[0]
    for k, out in enumerate((send0, send1, send2, send3)):
        out[...] = every[y ^ k]
    for fetch in fetches[needed:]:
        fetch.wait()


def forward_kernel(
    ids, x_ref, w_in_ref, b_in_ref, w_out_ref, b_out_ref,
    hidden_ref, slope_ref, send0, send2, send1, send3, values,
):
    step = pl.program_id(0)
    mem_dev, sub, _ = send0.shape
    pre = jnp.dot(x_ref[...], w_in_ref[...], preferred_element_type=F32) + b_in_ref[...]
    square = pre * pre
    t = jnp.tanh(pre * (GELU_C + (GELU_C * GELU_A) * square))
    half = 0.5 + 0.5 * t
    hidden = (pre * half).astype(BF16)
    hidden_ref[...] = hidden
    slope_ref[...] = half + pre * (0.5 - 0.5 * (t * t)) * (
        GELU_C + (3.0 * GELU_A * GELU_C) * square
    )
    part = lax.dot_general(
        hidden, w_out_ref[...], (((1,), (1,)), ((), ())), preferred_element_type=F32
    )

    @pl.when(step == 0)
    def _():
        values[...] = part + b_out_ref[...]

    @pl.when(step > 0)
    def _():
        values[...] += part

    @pl.when(step == pl.num_programs(0) - 1)
    def _():
        y = ids[0]
        for k, out in enumerate((send0, send1, send2, send3)):
            dest = y ^ k
            for m in range(mem_dev):
                start = pl.multiple_of(m * 4 * sub + dest * sub, sub)
                out[m] = values[pl.ds(start, sub), :].astype(BF16)


def loss_kernel(got0, got2, got1, got3, target_ref, weight_ref, loss_ref):
    gots = (got0, got1, got2, got3)
    mem_dev = got0.shape[0]
    n_mem = 4 * mem_dev
    epsil = (1.0 - ALPHA) / n_mem
    ens = [got[m].astype(F32) for got in gots for m in range(mem_dev)]
    truth = target_ref[...]
    skill = jnp.zeros_like(truth)
    spread = jnp.zeros_like(truth)
    for j in range(n_mem):
        skill = skill + jnp.abs(ens[j] - truth)
        for k in range(j):
            spread = spread + jnp.abs(ens[j] - ens[k])
    cell = weight_ref[...] * (skill / n_mem - (1.0 - epsil) / (n_mem * (n_mem - 1)) * spread)
    loss_ref[...] = jnp.zeros((8, 128), F32) + jnp.sum(cell)


def backward_kernel(
    ids, got0, got2, got1, got3, x_ref, hidden_ref, slope_ref, w_out_ref, bout_ref,
    keep_ref, send_ref, back, back_wide, small,
):
    mem_dev, sub, n_vars = got0.shape
    core = ids[2]
    hid = hidden_ref.shape[1]
    y = ids[0]
    for k, got in enumerate((got0, got1, got2, got3)):
        source = y ^ k
        for m in range(mem_dev):
            start = pl.multiple_of(m * 4 * sub + source * sub, sub)
            back[pl.ds(start, sub), :] = got[m]
    var = lax.broadcasted_iota(jnp.int32, (n_vars, 128), 0)
    lane = lax.broadcasted_iota(jnp.int32, (n_vars, 128), 1)
    place = jnp.where(lane == var + 3 * (var // PER_BLOCK), 1.0, 0.0).astype(BF16)
    back_wide[...] = jnp.dot(back[...], place, preferred_element_type=F32).astype(BF16)

    for start in range(0, hid, 256):
        cols = slice(start, start + 256)
        upward = jnp.dot(back[...], w_out_ref[:, cols], preferred_element_type=F32)
        dhidden = (upward * slope_ref[:, cols]).astype(BF16)
        small[:, cols] = lax.dot_general(
            back_wide[...], hidden_ref[:, cols], (((0,), (0,)), ((), ())), preferred_element_type=F32
        )
        small[ROW_BIN : ROW_BIN + 1, cols] = jnp.sum(dhidden.astype(F32), axis=0, keepdims=True)
        grad = lax.dot_general(
            x_ref[...], dhidden, (((0,), (0,)), ((), ())), preferred_element_type=F32
        )
        grad = grad.reshape(32, 2, 16, 256)
        first, second = grad[:, 0], grad[:, 1]
        keep_ref[:, :, cols] = jnp.where(core == 0, first, second)
        send_ref[:, :, cols] = jnp.where(core == 0, second, first).astype(BF16)

    small[ROW_BOUT : ROW_BOUT + 1, 0:n_vars] = bout_ref[...]
    for part in range(4):
        start = pl.multiple_of((2 * part + core) * 16, 16)
        rows = small[pl.ds(start, 16), :]
        for j in range(8):
            keep_ref[part * 8 + j, :, hid:] = rows[:, j * 128 : (j + 1) * 128]
        start = pl.multiple_of((2 * part + 1 - core) * 16, 16)
        rows = unfold(small[pl.ds(start, 16), :]).astype(BF16)
        for j in range(8):
            send_ref[part * 8 + j, :, hid:] = rows[:, j * 128 : (j + 1) * 128]


def payload_kernel(keep_ref, got_ref, out_hbm, out_ref, sems):
    n_plane, _, width = keep_ref.shape
    hid = width - 128
    piece = n_plane // 4
    stores = []
    for i in range(4):
        part = slice(i * piece, (i + 1) * piece)
        total = keep_ref[part, :, 0:hid] + got_ref[part, :, 0:hid].astype(F32)
        out_ref[part, :, 0:hid] = total.astype(BF16)
        for j in range(i * piece, (i + 1) * piece):
            block = unfold(keep_ref[j, :, hid:] + fold(got_ref[j, :, hid:].astype(F32)))
            out_ref[j, :, hid:] = block.astype(BF16)
        part = pl.ds(i * piece, piece)
        store = pltpu.make_async_copy(out_ref.at[part], out_hbm.at[part], sems.at[i])
        store.start()
        stores.append(store)
    for store in stores:
        store.wait()


def plane_kernel(ids, landed_ref, own_ref, small_ref, part2, part1, part3):
    hid = own_ref.shape[1]
    total = jnp.sum(landed_ref[...].astype(F32), axis=0)
    small = fold(total[:, hid:])
    small_ref[...] = small
    zhi = ids[1]
    quarters = [total[4 * z : 4 * z + 4, 0:hid] for z in range(4)]

    def quarter(which):
        out = quarters[3]
        for z in range(3):
            out = jnp.where(which == z, quarters[z], out)
        return out

    own_ref[...] = quarter(zhi)
    for k, out in ((1, part1), (2, part2), (3, part3)):
        rows = quarter(lax.rem(zhi + k, 4))
        for j in range(4):
            out[4 * j : 4 * j + 4, 0:256] = rows[:, j * 256 : (j + 1) * 256]
        out[:, 256:384] = small


def total_kernel(ids, own_ref, small_ref, got2, got1, got3, loss_ref, grad_ref, copies_ref):
    zhi = ids[1]
    for j in range(4):
        acc = own_ref[:, j * 256 : (j + 1) * 256]
        for got in (got1, got2, got3):
            acc = acc + got[4 * j : 4 * j + 4, 0:256]
        grad_ref[:, j * 256 : (j + 1) * 256] = acc
    parts = [small_ref[...]] + [got[:, 256:384] for got in (got1, got2, got3)]
    acc = None
    for source in range(4):
        term = parts[0]
        for k in range(1, 4):
            term = jnp.where(lax.rem(zhi + 4 - k, 4) == source, parts[k], term)
        acc = term if acc is None else acc + term
    row = lax.broadcasted_iota(jnp.int32, acc.shape, 0)
    acc = jnp.where(row == ROW_LOSS, loss_ref[0:1, :], acc)
    copies_ref[...] = jnp.broadcast_to(acc[None], copies_ref.shape)


def final_kernel(
    scale, loss_scale, ids, grad_ref, mine, theirs,
    in_hbm, out_hbm, bin_hbm, bout_hbm, loss_hbm,
    full, in_ref, out_ref, bin_ref, bout_ref, loss_ref, sems,
):
    core = ids[2]
    n_vars = out_ref.shape[0]
    stores = []

    def store(source, target):
        copy = pltpu.make_async_copy(source, target, sems.at[len(stores)])
        copy.start()
        stores.append(copy)

    in_ref[...] = grad_ref[...] * scale
    store(in_ref, in_hbm)
    for which, blocks in ((core, mine), (1 - core, theirs)):
        for part in range(4):
            start = pl.multiple_of((2 * part + which) * 16, 16)
            for j in range(8):
                full[pl.ds(start, 16), j * 128 : (j + 1) * 128] = blocks[part * 8 + j]
    for q in range(8):
        count = min(PER_BLOCK, n_vars - PER_BLOCK * q)
        out_ref[PER_BLOCK * q : PER_BLOCK * q + count, :] = full[16 * q : 16 * q + count, :] * scale
        if q == 3:
            store(out_ref.at[0:48, :], out_hbm.at[0:48, :])
    store(out_ref.at[48:n_vars, :], out_hbm.at[48:n_vars, :])
    bin_ref[...] = full[ROW_BIN : ROW_BIN + 1, :] * scale
    store(bin_ref, bin_hbm)
    bout_ref[...] = full[ROW_BOUT : ROW_BOUT + 1, 0:n_vars] * scale
    store(bout_ref, bout_hbm)
    total = jnp.zeros((1, 128), F32)
    for q in range(8):
        for j in range(8):
            total = total + full[16 * q + ROW_LOSS : 16 * q + ROW_LOSS + 1, 128 * j : 128 * (j + 1)]
    loss_ref[...] = total[:, 0:1] * loss_scale
    store(loss_ref, loss_hbm)
    for copy in stores:
        copy.wait()


def per_device(latents, w_in, b_in, w_out, b_out, targets, area, var_weight, member_rank, obs_rank):
    mem_dev = latents.shape[1]
    pts_dev = latents.shape[2]
    width = latents.shape[3]
    hid = w_in.shape[1]
    n_vars = w_out.shape[1]
    n_y = lax.axis_size("y")
    n_mem = mem_dev * n_y
    sub = pts_dev // n_y
    rows = mem_dev * pts_dev
    n_points = pts_dev * lax.axis_size(GRID)
    scale = 1.0 / math.sqrt(lax.axis_size("zhi") * n_mem * n_points)
    ids = jnp.stack(
        [lax.axis_index("y"), lax.axis_index("zhi"), lax.axis_index("core")]
    ).astype(jnp.int32)
    shape = jax.ShapeDtypeStruct

    x = latents.reshape(rows, width)
    w_out_t = w_out.T
    ranks = member_rank[0].transpose(0, 2, 1)
    obs = obs_rank[0].T
    truth = targets[0].T
    sent = shape((mem_dev, sub, n_vars), BF16)
    whole = pl.BlockSpec(memory_space=pltpu.VMEM)

    hbm = pl.BlockSpec(memory_space=pltpu.HBM)
    operands = [
        pltpu.with_memory_space_constraint(arr, pltpu.HBM)
        for arr in (
            ranks, obs, area[None, :], var_weight[None, :],
            x, w_in, b_in[None, :], w_out_t, b_out[None, :],
        )
    ]
    weight, bout, cot0, cot2, cot1, cot3, x, w_in, b_in, w_out_t, b_out = pl.pallas_call(
        cotangent_kernel,
        in_specs=[SMEM] + [hbm] * 9,
        out_specs=[whole] * 11,
        out_shape=[shape((sub, n_vars), F32), shape((1, n_vars), F32)]
        + [sent] * 4
        + [
            shape((rows, width), BF16),
            shape((width, hid), BF16),
            shape((1, hid), F32),
            shape((n_vars, hid), BF16),
            shape((1, n_vars), F32),
        ],
        scratch_shapes=[
            pltpu.VMEM((n_y, mem_dev, sub, n_vars), BF16),
            pltpu.VMEM((n_mem, sub, n_vars), jnp.int32),
            pltpu.VMEM((sub, n_vars), jnp.int32),
            pltpu.VMEM((1, sub), F32),
            pltpu.VMEM((1, n_vars), F32),
            pltpu.SemaphoreType.DMA((15,)),
        ],
        compiler_params=PARAMS,
        name="cotangent",
    )(ids, *operands)
    ids_later, cot2, cot1, cot3 = lax.optimization_barrier((ids, cot2, cot1, cot3))
    cot2 = lax.ppermute(cot2, "y", pairs_of("y", 2))
    cot1 = lax.ppermute(cot1, "y", pairs_of("y", 1))
    cot3 = lax.ppermute(cot3, "y", pairs_of("y", 3))

    cols = 512
    by_cols = lambda height: pl.BlockSpec((height, cols), lambda i: (0, i))
    hidden, slope, val0, val2, val1, val3 = pl.pallas_call(
        forward_kernel,
        grid=(hid // cols,),
        in_specs=[
            SMEM,
            const_spec((rows, width)),
            by_cols(width),
            by_cols(1),
            by_cols(n_vars),
            const_spec((1, n_vars)),
        ],
        out_specs=[by_cols(rows), by_cols(rows)] + [const_spec(sent.shape)] * 4,
        out_shape=[shape((rows, hid), BF16), shape((rows, hid), F32)] + [sent] * 4,
        scratch_shapes=[pltpu.VMEM((rows, n_vars), F32)],
        compiler_params=PARAMS,
        name="forward",
    )(ids_later, x, w_in, b_in, w_out_t, b_out)

    n_plane = lax.axis_size(PLANE)
    block = width // (2 * n_plane)
    keep, send = pl.pallas_call(
        backward_kernel,
        in_specs=[SMEM] + [whole] * 9,
        out_specs=[whole] * 2,
        out_shape=[
            shape((n_plane, block, hid + 128), F32),
            shape((n_plane, block, hid + 128), BF16),
        ],
        scratch_shapes=[
            pltpu.VMEM((rows, n_vars), BF16),
            pltpu.VMEM((rows, 128), BF16),
            pltpu.VMEM((128, hid), F32),
        ],
        compiler_params=PARAMS,
        name="backward",
    )(ids, cot0, cot2, cot1, cot3, x, hidden, slope, w_out_t, bout)

    swap = [(0, 1), (1, 0)]
    got = lax.ppermute(send, "core", swap)
    payload_shape = (n_plane, block, hid + 128)
    payload = pl.pallas_call(
        payload_kernel,
        in_specs=[whole] * 2,
        out_specs=hbm,
        out_shape=shape(payload_shape, BF16),
        scratch_shapes=[pltpu.VMEM(payload_shape, BF16), pltpu.SemaphoreType.DMA((4,))],
        compiler_params=PARAMS,
        name="payload",
    )(keep, got)
    payload, val2, val1, val3 = lax.optimization_barrier((payload, val2, val1, val3))
    landed = lax.all_to_all(payload, PLANE, 0, 0, tiled=True)
    val2 = lax.ppermute(val2, "y", pairs_of("y", 2))
    val1 = lax.ppermute(val1, "y", pairs_of("y", 1))
    val3 = lax.ppermute(val3, "y", pairs_of("y", 3))
    part_loss = pl.pallas_call(
        loss_kernel,
        in_specs=[whole] * 6,
        out_specs=whole,
        out_shape=shape((8, 128), F32),
        compiler_params=PARAMS,
        name="loss",
    )(val0, val2, val1, val3, truth, weight)

    part = shape((block, 384), F32)
    own, small, part2, part1, part3 = pl.pallas_call(
        plane_kernel,
        in_specs=[SMEM, whole],
        out_specs=[whole] * 5,
        out_shape=[shape((block // 4, hid), F32), shape((block, 128), F32), part, part, part],
        compiler_params=PARAMS,
        name="plane_sum",
    )(ids, landed)
    part2 = lax.ppermute(part2, "zhi", shift("zhi", 2))
    part1 = lax.ppermute(part1, "zhi", shift("zhi", 1))
    part3 = lax.ppermute(part3, "zhi", shift("zhi", 3))
    grad_in, copies = pl.pallas_call(
        total_kernel,
        in_specs=[SMEM] + [whole] * 6,
        out_specs=[whole] * 2,
        out_shape=[shape((block // 4, hid), F32), shape((n_plane, block, 128), F32)],
        compiler_params=PARAMS,
        name="total",
    )(ids, own, small, part2, part1, part3, part_loss)

    mine = lax.all_to_all(copies, PLANE, 0, 0, tiled=True)
    theirs = lax.ppermute(mine, "core", swap)
    finals = [
        shape((block // 4, hid), F32),
        shape((n_vars, hid), F32),
        shape((1, hid), F32),
        shape((1, n_vars), F32),
        shape((1, 1), F32),
    ]
    grad_in, grad_out, grad_bin, grad_bout, loss = pl.pallas_call(
        lambda *refs: final_kernel(scale, 1.0 / (n_points * n_vars), *refs),
        in_specs=[SMEM] + [whole] * 3,
        out_specs=[hbm] * 5,
        out_shape=finals,
        scratch_shapes=[pltpu.VMEM((128, hid), F32)]
        + [pltpu.VMEM(final.shape, F32) for final in finals]
        + [pltpu.SemaphoreType.DMA((6,))],
        compiler_params=PARAMS,
        name="unpack",
    )(ids, grad_in, mine, theirs)
    return (loss.reshape(1), grad_in, grad_out.T, grad_bin.reshape(hid), grad_bout.reshape(n_vars))


def solution(mesh):
    split = Mesh(mesh.devices.reshape(4, 2, 4, 2, 4), NAMES)
    points = GRID + ("y",)
    in_specs = (
        P("zhi", "y", GRID, None),
        P(),
        P(),
        P(),
        P(),
        P("zhi", None, points),
        P(points),
        P(),
        P("zhi", None, None, points),
        P("zhi", None, points),
    )
    out_specs = (P("zhi"), P(NAMES, None), P(), P(), P())
    return jax.shard_map(
        per_device, mesh=split, in_specs=in_specs, out_specs=out_specs, check_vma=False
    )
```

```python
import math

import jax
import jax.numpy as jnp
from jax import lax
from jax.experimental import pallas as pl
from jax.experimental.pallas import tpu as pltpu
from jax.sharding import Mesh
from jax.sharding import PartitionSpec as P

ALPHA = 0.95
NAMES = ("y", "zlo", "x", "core", "zhi")
PLANE = ("y", "zlo", "x")
GRID = ("zlo", "x", "core")
F32 = jnp.float32
BF16 = jnp.bfloat16
GELU_C = math.sqrt(2.0 / math.pi)
GELU_A = 0.044715
PARAMS = pltpu.CompilerParams(vmem_limit_bytes=24 * 1024 * 1024)
SMEM = pl.BlockSpec(memory_space=pltpu.SMEM)

PER_BLOCK = 13
ROW_BIN, ROW_BOUT, ROW_LOSS = 121, 122, 15


def shift(axis, step):
    size = lax.axis_size(axis)
    return [(i, (i + step) % size) for i in range(size)]


def pairs_of(axis, step):
    return [(i, i ^ step) for i in range(lax.axis_size(axis))]


def const_spec(shape):
    return pl.BlockSpec(shape, lambda *_: (0,) * len(shape))


def fold(block):
    row = lax.broadcasted_iota(jnp.int32, block.shape, 0)
    up = pltpu.roll(block, 12, 0)
    low = (row == 13) | (row == 14)
    return jnp.where((row == 9) | (row == 10), block + up, jnp.where(low, 0.0, block))


def unfold(block):
    row = lax.broadcasted_iota(jnp.int32, block.shape, 0)
    low = block - block.astype(BF16).astype(F32)
    return jnp.where((row == 13) | (row == 14), pltpu.roll(low, 4, 0), block)


def cotangent_kernel(
    ids, rank_hbm, obs_hbm, area_hbm, vw_hbm, x_hbm, w_in_hbm, b_in_hbm, w_out_hbm, b_out_hbm,
    weight_ref, bout_ref, send0, send2, send1, send3, x_ref, w_in_ref, b_in_ref, w_out_ref, b_out_ref,
    every, rank_ref, obs_ref, area_ref, vw_ref, sems,
):
    pairs = [(rank_hbm, rank_ref), (obs_hbm, obs_ref), (area_hbm, area_ref), (vw_hbm, vw_ref)]
    needed = len(pairs)
    pairs += [(w_out_hbm, w_out_ref), (b_in_hbm, b_in_ref), (b_out_hbm, b_out_ref)]
    for source, target in ((x_hbm, x_ref), (w_in_hbm, w_in_ref)):
        piece = source.shape[0] // 4
        for i in range(4):
            rows = pl.ds(i * piece, piece)
            pairs.append((source.at[rows, :], target.at[rows, :]))
    fetches = [
        pltpu.make_async_copy(source, target, sems.at[i]) for i, (source, target) in enumerate(pairs)
    ]
    for fetch in fetches:
        fetch.start()
    for fetch in fetches[:needed]:
        fetch.wait()
    n_mem, sub, n_vars = rank_ref.shape
    mem_dev = n_mem // 4
    epsil = (1.0 - ALPHA) / n_mem
    row = lax.broadcasted_iota(jnp.int32, (sub, sub), 0)
    lane = lax.broadcasted_iota(jnp.int32, (sub, sub), 1)
    area = jnp.sum(jnp.where(row == lane, area_ref[...], 0.0), axis=1, keepdims=True)
    weight = area * vw_ref[...]
    weight_ref[...] = weight
    obs = obs_ref[...]
    total = jnp.zeros_like(weight)
    for member in range(n_mem):
        rank = rank_ref[member]
        sign = jnp.where(rank >= obs, 1.0, -1.0)
        centred = (2 * rank - n_mem + 1).astype(F32)
        cot = (weight * (sign - (1.0 - epsil) / (n_mem - 1) * centred)).astype(BF16)
        every[member // mem_dev, member % mem_dev] = cot
        total = total + cot.astype(F32)
    bout_ref[...] = jnp.sum(total, axis=0, keepdims=True)
    y = ids[0]
    for k, out in enumerate((send0, send1, send2, send3)):
        out[...] = every[y ^ k]
    for fetch in fetches[needed:]:
        fetch.wait()


def forward_kernel(
    ids, x_ref, w_in_ref, b_in_ref, w_out_ref, b_out_ref,
    hidden_ref, slope_ref, send0, send2, send1, send3, values,
):
    step = pl.program_id(0)
    mem_dev, sub, _ = send0.shape
    pre = jnp.dot(x_ref[...], w_in_ref[...], preferred_element_type=F32) + b_in_ref[...]
    square = pre * pre
    t = jnp.tanh(pre * (GELU_C + (GELU_C * GELU_A) * square))
    half = 0.5 + 0.5 * t
    hidden = (pre * half).astype(BF16)
    hidden_ref[...] = hidden
    slope_ref[...] = half + pre * (0.5 - 0.5 * (t * t)) * (
        GELU_C + (3.0 * GELU_A * GELU_C) * square
    )
    part = lax.dot_general(
        hidden, w_out_ref[...], (((1,), (1,)), ((), ())), preferred_element_type=F32
    )

    @pl.when(step == 0)
    def _():
        values[...] = part + b_out_ref[...]

    @pl.when(step > 0)
    def _():
        values[...] += part

    @pl.when(step == pl.num_programs(0) - 1)
    def _():
        y = ids[0]
        for k, out in enumerate((send0, send1, send2, send3)):
            dest = y ^ k
            for m in range(mem_dev):
                start = pl.multiple_of(m * 4 * sub + dest * sub, sub)
                out[m] = values[pl.ds(start, sub), :].astype(BF16)


def loss_kernel(got0, got2, got1, got3, target_ref, weight_ref, loss_ref):
    gots = (got0, got1, got2, got3)
    mem_dev = got0.shape[0]
    n_mem = 4 * mem_dev
    epsil = (1.0 - ALPHA) / n_mem
    ens = [got[m].astype(F32) for got in gots for m in range(mem_dev)]
    truth = target_ref[...]
    skill = jnp.zeros_like(truth)
    spread = jnp.zeros_like(truth)
    for j in range(n_mem):
        skill = skill + jnp.abs(ens[j] - truth)
        for k in range(j):
            spread = spread + jnp.abs(ens[j] - ens[k])
    cell = weight_ref[...] * (skill / n_mem - (1.0 - epsil) / (n_mem * (n_mem - 1)) * spread)
    loss_ref[...] = jnp.zeros((8, 128), F32) + jnp.sum(cell)


def backward_kernel(
    ids, got0, got2, got1, got3, x_ref, hidden_ref, slope_ref, w_out_ref, bout_ref,
    keep_ref, send_ref, back, back_wide, small,
):
    mem_dev, sub, n_vars = got0.shape
    core = ids[2]
    hid = hidden_ref.shape[1]
    y = ids[0]
    for k, got in enumerate((got0, got1, got2, got3)):
        source = y ^ k
        for m in range(mem_dev):
            start = pl.multiple_of(m * 4 * sub + source * sub, sub)
            back[pl.ds(start, sub), :] = got[m]
    var = lax.broadcasted_iota(jnp.int32, (n_vars, 128), 0)
    lane = lax.broadcasted_iota(jnp.int32, (n_vars, 128), 1)
    place = jnp.where(lane == var + 3 * (var // PER_BLOCK), 1.0, 0.0).astype(BF16)
    back_wide[...] = jnp.dot(back[...], place, preferred_element_type=F32).astype(BF16)

    for start in range(0, hid, 256):
        cols = slice(start, start + 256)
        upward = jnp.dot(back[...], w_out_ref[:, cols], preferred_element_type=F32)
        dhidden = (upward * slope_ref[:, cols]).astype(BF16)
        small[:, cols] = lax.dot_general(
            back_wide[...], hidden_ref[:, cols], (((0,), (0,)), ((), ())), preferred_element_type=F32
        )
        small[ROW_BIN : ROW_BIN + 1, cols] = jnp.sum(dhidden.astype(F32), axis=0, keepdims=True)
        grad = lax.dot_general(
            x_ref[...], dhidden, (((0,), (0,)), ((), ())), preferred_element_type=F32
        )
        grad = grad.reshape(32, 2, 16, 256)
        first, second = grad[:, 0], grad[:, 1]
        keep_ref[:, :, cols] = jnp.where(core == 0, first, second)
        send_ref[:, :, cols] = jnp.where(core == 0, second, first).astype(BF16)

    small[ROW_BOUT : ROW_BOUT + 1, 0:n_vars] = bout_ref[...]
    for part in range(4):
        start = pl.multiple_of((2 * part + core) * 16, 16)
        rows = small[pl.ds(start, 16), :]
        for j in range(8):
            keep_ref[part * 8 + j, :, hid:] = rows[:, j * 128 : (j + 1) * 128]
        start = pl.multiple_of((2 * part + 1 - core) * 16, 16)
        rows = unfold(small[pl.ds(start, 16), :]).astype(BF16)
        for j in range(8):
            send_ref[part * 8 + j, :, hid:] = rows[:, j * 128 : (j + 1) * 128]


def payload_kernel(keep_ref, got_ref, out_hbm, out_ref, sems):
    n_plane, _, width = keep_ref.shape
    hid = width - 128
    first = hid // 2
    piece = n_plane // 4
    stores = []
    for i in range(4):
        part = slice(i * piece, (i + 1) * piece)
        total = keep_ref[part, :, 0:first] + got_ref[part, :, 0:first].astype(F32)
        out_ref[part, :, 0:first] = total.astype(BF16)
        for j in range(i * piece, (i + 1) * piece):
            block = unfold(keep_ref[j, :, hid:] + fold(got_ref[j, :, hid:].astype(F32)))
            out_ref[j, :, first:] = block.astype(BF16)
        part = pl.ds(i * piece, piece)
        store = pltpu.make_async_copy(out_ref.at[part], out_hbm.at[part], sems.at[i])
        store.start()
        stores.append(store)
    for store in stores:
        store.wait()


def second_half_kernel(ids, keep_ref, got_ref, own_ref, part2, part1, part3, quarters):
    n_plane = keep_ref.shape[0]
    first = own_ref.shape[1]
    zhi = ids[1]
    for n in range(n_plane):
        total = keep_ref[n, :, first : 2 * first] + got_ref[n, :, first : 2 * first].astype(F32)
        for z in range(4):
            quarters[lax.rem(z + 4 - zhi, 4), 4 * n : 4 * n + 4, :] = total[4 * z : 4 * z + 4, :]
    own_ref[...] = quarters[0]
    part1[...] = quarters[1].astype(BF16)
    part2[...] = quarters[2].astype(BF16)
    part3[...] = quarters[3].astype(BF16)


def second_total_kernel(own_ref, got2, got1, got3, out_ref, total, wide):
    n_plane = out_ref.shape[0]
    total[...] = own_ref[...] + got1[...].astype(F32) + got2[...].astype(F32) + got3[...].astype(F32)
    for n in range(n_plane):
        for j in range(4):
            wide[n, 4 * j : 4 * j + 4, :] = total[4 * n : 4 * n + 4, 128 * j : 128 * (j + 1)]
    out_ref[...] = wide[...].astype(BF16)


def plane_kernel(ids, landed_ref, own_ref, small_ref, part2, part1, part3):
    first = own_ref.shape[1]
    total = jnp.sum(landed_ref[...].astype(F32), axis=0)
    small = fold(total[:, first:])
    small_ref[...] = small
    zhi = ids[1]
    quarters = [total[4 * z : 4 * z + 4, 0:first] for z in range(4)]

    def quarter(which):
        out = quarters[3]
        for z in range(3):
            out = jnp.where(which == z, quarters[z], out)
        return out

    own_ref[...] = quarter(zhi)
    for k, out in ((1, part1), (2, part2), (3, part3)):
        rows = quarter(lax.rem(zhi + k, 4))
        for j in range(4):
            out[4 * j : 4 * j + 4, 0:128] = rows[:, j * 128 : (j + 1) * 128]
        out[:, 128:256] = small


def total_kernel(ids, own_ref, small_ref, got2, got1, got3, loss_ref, second_ref, grad_ref, copies_ref):
    zhi = ids[1]
    for j in range(4):
        acc = own_ref[:, j * 128 : (j + 1) * 128]
        for got in (got1, got2, got3):
            acc = acc + got[4 * j : 4 * j + 4, 0:128]
        grad_ref[:, j * 128 : (j + 1) * 128] = acc
    parts = [small_ref[...]] + [got[:, 128:256] for got in (got1, got2, got3)]
    acc = None
    for source in range(4):
        term = parts[0]
        for k in range(1, 4):
            term = jnp.where(lax.rem(zhi + 4 - k, 4) == source, parts[k], term)
        acc = term if acc is None else acc + term
    row = lax.broadcasted_iota(jnp.int32, acc.shape, 0)
    acc = jnp.where(row == ROW_LOSS, loss_ref[0:1, :], acc)
    high = acc.astype(BF16)
    low = (acc - high.astype(F32)).astype(BF16)
    count = copies_ref.shape[0]
    copies_ref[:, 0:16, :] = jnp.broadcast_to(high[None], (count, 16, 128))
    copies_ref[:, 16:32, :] = jnp.broadcast_to(low[None], (count, 16, 128))
    copies_ref[:, 32:48, :] = second_ref[...]


def final_kernel(
    scale, loss_scale, ids, grad_ref, mine, theirs,
    in_hbm, out_hbm, bin_hbm, bout_hbm, loss_hbm,
    full, in_ref, out_ref, bin_ref, bout_ref, loss_ref, sems,
):
    core = ids[2]
    n_vars = out_ref.shape[0]
    stores = []

    def store(source, target):
        copy = pltpu.make_async_copy(source, target, sems.at[len(stores)])
        copy.start()
        stores.append(copy)

    first = grad_ref.shape[1]
    in_ref[:, 0:first] = grad_ref[...] * scale
    second = jnp.sum(mine[:, 32:48, :].astype(F32), axis=0) * scale
    for j in range(4):
        start = first + 128 * j
        in_ref[:, start : start + 128] = second[4 * j : 4 * j + 4, :]
    store(in_ref, in_hbm)
    for which, blocks in ((core, mine), (1 - core, theirs)):
        for part in range(4):
            start = pl.multiple_of((2 * part + which) * 16, 16)
            for j in range(8):
                block = blocks[part * 8 + j, 0:16, :].astype(F32)
                block = block + blocks[part * 8 + j, 16:32, :].astype(F32)
                full[pl.ds(start, 16), j * 128 : (j + 1) * 128] = block
    for q in range(8):
        count = min(PER_BLOCK, n_vars - PER_BLOCK * q)
        out_ref[PER_BLOCK * q : PER_BLOCK * q + count, :] = full[16 * q : 16 * q + count, :] * scale
        if q == 3:
            store(out_ref.at[0:48, :], out_hbm.at[0:48, :])
    store(out_ref.at[48:n_vars, :], out_hbm.at[48:n_vars, :])
    bin_ref[...] = full[ROW_BIN : ROW_BIN + 1, :] * scale
    store(bin_ref, bin_hbm)
    bout_ref[...] = full[ROW_BOUT : ROW_BOUT + 1, 0:n_vars] * scale
    store(bout_ref, bout_hbm)
    total = jnp.zeros((1, 128), F32)
    for q in range(8):
        for j in range(8):
            total = total + full[16 * q + ROW_LOSS : 16 * q + ROW_LOSS + 1, 128 * j : 128 * (j + 1)]
    loss_ref[...] = total[:, 0:1] * loss_scale
    store(loss_ref, loss_hbm)
    for copy in stores:
        copy.wait()


def per_device(latents, w_in, b_in, w_out, b_out, targets, area, var_weight, member_rank, obs_rank):
    mem_dev = latents.shape[1]
    pts_dev = latents.shape[2]
    width = latents.shape[3]
    hid = w_in.shape[1]
    n_vars = w_out.shape[1]
    n_y = lax.axis_size("y")
    n_mem = mem_dev * n_y
    sub = pts_dev // n_y
    rows = mem_dev * pts_dev
    n_points = pts_dev * lax.axis_size(GRID)
    scale = 1.0 / math.sqrt(lax.axis_size("zhi") * n_mem * n_points)
    ids = jnp.stack(
        [lax.axis_index("y"), lax.axis_index("zhi"), lax.axis_index("core")]
    ).astype(jnp.int32)
    shape = jax.ShapeDtypeStruct

    x = latents.reshape(rows, width)
    w_out_t = w_out.T
    ranks = member_rank[0].transpose(0, 2, 1)
    obs = obs_rank[0].T
    truth = targets[0].T
    sent = shape((mem_dev, sub, n_vars), BF16)
    whole = pl.BlockSpec(memory_space=pltpu.VMEM)

    hbm = pl.BlockSpec(memory_space=pltpu.HBM)
    operands = [
        pltpu.with_memory_space_constraint(arr, pltpu.HBM)
        for arr in (
            ranks, obs, area[None, :], var_weight[None, :],
            x, w_in, b_in[None, :], w_out_t, b_out[None, :],
        )
    ]
    weight, bout, cot0, cot2, cot1, cot3, x, w_in, b_in, w_out_t, b_out = pl.pallas_call(
        cotangent_kernel,
        in_specs=[SMEM] + [hbm] * 9,
        out_specs=[whole] * 11,
        out_shape=[shape((sub, n_vars), F32), shape((1, n_vars), F32)]
        + [sent] * 4
        + [
            shape((rows, width), BF16),
            shape((width, hid), BF16),
            shape((1, hid), F32),
            shape((n_vars, hid), BF16),
            shape((1, n_vars), F32),
        ],
        scratch_shapes=[
            pltpu.VMEM((n_y, mem_dev, sub, n_vars), BF16),
            pltpu.VMEM((n_mem, sub, n_vars), jnp.int32),
            pltpu.VMEM((sub, n_vars), jnp.int32),
            pltpu.VMEM((1, sub), F32),
            pltpu.VMEM((1, n_vars), F32),
            pltpu.SemaphoreType.DMA((15,)),
        ],
        compiler_params=PARAMS,
        name="cotangent",
    )(ids, *operands)
    ids_later, cot2, cot1, cot3 = lax.optimization_barrier((ids, cot2, cot1, cot3))
    cot2 = lax.ppermute(cot2, "y", pairs_of("y", 2))
    cot1 = lax.ppermute(cot1, "y", pairs_of("y", 1))
    cot3 = lax.ppermute(cot3, "y", pairs_of("y", 3))

    cols = 512
    by_cols = lambda height: pl.BlockSpec((height, cols), lambda i: (0, i))
    hidden, slope, val0, val2, val1, val3 = pl.pallas_call(
        forward_kernel,
        grid=(hid // cols,),
        in_specs=[
            SMEM,
            const_spec((rows, width)),
            by_cols(width),
            by_cols(1),
            by_cols(n_vars),
            const_spec((1, n_vars)),
        ],
        out_specs=[by_cols(rows), by_cols(rows)] + [const_spec(sent.shape)] * 4,
        out_shape=[shape((rows, hid), BF16), shape((rows, hid), F32)] + [sent] * 4,
        scratch_shapes=[pltpu.VMEM((rows, n_vars), F32)],
        compiler_params=PARAMS,
        name="forward",
    )(ids_later, x, w_in, b_in, w_out_t, b_out)

    n_plane = lax.axis_size(PLANE)
    block = width // (2 * n_plane)
    keep, send = pl.pallas_call(
        backward_kernel,
        in_specs=[SMEM] + [whole] * 9,
        out_specs=[whole] * 2,
        out_shape=[
            shape((n_plane, block, hid + 128), F32),
            shape((n_plane, block, hid + 128), BF16),
        ],
        scratch_shapes=[
            pltpu.VMEM((rows, n_vars), BF16),
            pltpu.VMEM((rows, 128), BF16),
            pltpu.VMEM((128, hid), F32),
        ],
        compiler_params=PARAMS,
        name="backward",
    )(ids, cot0, cot2, cot1, cot3, x, hidden, slope, w_out_t, bout)

    swap = [(0, 1), (1, 0)]
    got = lax.ppermute(send, "core", swap)
    first = hid // 2
    payload_shape = (n_plane, block, first + 128)
    payload = pl.pallas_call(
        payload_kernel,
        in_specs=[whole] * 2,
        out_specs=hbm,
        out_shape=shape(payload_shape, BF16),
        scratch_shapes=[pltpu.VMEM(payload_shape, BF16), pltpu.SemaphoreType.DMA((4,))],
        compiler_params=PARAMS,
        name="payload",
    )(keep, got)
    payload, keep, got, val2, val1, val3 = lax.optimization_barrier(
        (payload, keep, got, val2, val1, val3)
    )
    landed = lax.all_to_all(payload, PLANE, 0, 0, tiled=True)

    n_rows = n_plane * block // 4
    quarter = shape((n_rows, first), BF16)
    own_second, second2, second1, second3 = pl.pallas_call(
        second_half_kernel,
        in_specs=[SMEM, whole, whole],
        out_specs=[whole] * 4,
        out_shape=[shape((n_rows, first), F32), quarter, quarter, quarter],
        scratch_shapes=[pltpu.VMEM((4, n_rows, first), F32)],
        compiler_params=PARAMS,
        name="second_half",
    )(ids, keep, got)
    second2 = lax.ppermute(second2, "zhi", shift("zhi", 2))
    second1 = lax.ppermute(second1, "zhi", shift("zhi", 1))
    second3 = lax.ppermute(second3, "zhi", shift("zhi", 3))
    val2 = lax.ppermute(val2, "y", pairs_of("y", 2))
    val1 = lax.ppermute(val1, "y", pairs_of("y", 1))
    val3 = lax.ppermute(val3, "y", pairs_of("y", 3))
    part_loss = pl.pallas_call(
        loss_kernel,
        in_specs=[whole] * 6,
        out_specs=whole,
        out_shape=shape((8, 128), F32),
        compiler_params=PARAMS,
        name="loss",
    )(val0, val2, val1, val3, truth, weight)
    second = pl.pallas_call(
        second_total_kernel,
        in_specs=[whole] * 4,
        out_specs=whole,
        out_shape=shape((n_plane, block, 128), BF16),
        scratch_shapes=[pltpu.VMEM((n_rows, first), F32), pltpu.VMEM((n_plane, block, 128), F32)],
        compiler_params=PARAMS,
        name="second_total",
    )(own_second, second2, second1, second3)

    part = shape((block, 256), F32)
    own, small, part2, part1, part3 = pl.pallas_call(
        plane_kernel,
        in_specs=[SMEM, whole],
        out_specs=[whole] * 5,
        out_shape=[shape((block // 4, first), F32), shape((block, 128), F32), part, part, part],
        compiler_params=PARAMS,
        name="plane_sum",
    )(ids, landed)
    part2 = lax.ppermute(part2, "zhi", shift("zhi", 2))
    part1 = lax.ppermute(part1, "zhi", shift("zhi", 1))
    part3 = lax.ppermute(part3, "zhi", shift("zhi", 3))
    grad_in, copies = pl.pallas_call(
        total_kernel,
        in_specs=[SMEM] + [whole] * 7,
        out_specs=[whole] * 2,
        out_shape=[shape((block // 4, first), F32), shape((n_plane, 3 * block, 128), BF16)],
        compiler_params=PARAMS,
        name="total",
    )(ids, own, small, part2, part1, part3, part_loss, second)

    mine = lax.all_to_all(copies, PLANE, 0, 0, tiled=True)
    theirs = lax.ppermute(mine, "core", swap)
    finals = [
        shape((block // 4, hid), F32),
        shape((n_vars, hid), F32),
        shape((1, hid), F32),
        shape((1, n_vars), F32),
        shape((1, 1), F32),
    ]
    grad_in, grad_out, grad_bin, grad_bout, loss = pl.pallas_call(
        lambda *refs: final_kernel(scale, 1.0 / (n_points * n_vars), *refs),
        in_specs=[SMEM] + [whole] * 3,
        out_specs=[hbm] * 5,
        out_shape=finals,
        scratch_shapes=[pltpu.VMEM((128, hid), F32)]
        + [pltpu.VMEM(final.shape, F32) for final in finals]
        + [pltpu.SemaphoreType.DMA((6,))],
        compiler_params=PARAMS,
        name="unpack",
    )(ids, grad_in, mine, theirs)
    return (loss.reshape(1), grad_in, grad_out.T, grad_bin.reshape(hid), grad_bout.reshape(n_vars))


def solution(mesh):
    split = Mesh(mesh.devices.reshape(4, 2, 4, 2, 4), NAMES)
    points = GRID + ("y",)
    in_specs = (
        P("zhi", "y", GRID, None),
        P(),
        P(),
        P(),
        P(),
        P("zhi", None, points),
        P(points),
        P(),
        P("zhi", None, None, points),
        P("zhi", None, points),
    )
    out_specs = (P("zhi"), P(NAMES, None), P(), P(), P())
    return jax.shard_map(
        per_device, mesh=split, in_specs=in_specs, out_specs=out_specs, check_vma=False
    )
```

```python
import math

import jax
import jax.numpy as jnp
from jax import lax
from jax.experimental import pallas as pl
from jax.experimental.pallas import tpu as pltpu
from jax.sharding import Mesh
from jax.sharding import PartitionSpec as P

ALPHA = 0.95
NAMES = ("y", "zlo", "x", "core", "zhi")
PLANE = ("y", "zlo", "x")
GRID = ("zlo", "x", "core")
F32 = jnp.float32
BF16 = jnp.bfloat16
GELU_C = math.sqrt(2.0 / math.pi)
GELU_A = 0.044715
PARAMS = pltpu.CompilerParams(vmem_limit_bytes=24 * 1024 * 1024)
SMEM = pl.BlockSpec(memory_space=pltpu.SMEM)

PER_BLOCK = 13
ROW_BIN, ROW_BOUT, ROW_LOSS = 121, 122, 15


def shift(axis, step):
    size = lax.axis_size(axis)
    return [(i, (i + step) % size) for i in range(size)]


def pairs_of(axis, step):
    return [(i, i ^ step) for i in range(lax.axis_size(axis))]


def const_spec(shape):
    return pl.BlockSpec(shape, lambda *_: (0,) * len(shape))


def fold(block):
    row = lax.broadcasted_iota(jnp.int32, block.shape, 0)
    up = pltpu.roll(block, 12, 0)
    low = (row == 13) | (row == 14)
    return jnp.where((row == 9) | (row == 10), block + up, jnp.where(low, 0.0, block))


def unfold(block):
    row = lax.broadcasted_iota(jnp.int32, block.shape, 0)
    low = block - block.astype(BF16).astype(F32)
    return jnp.where((row == 13) | (row == 14), pltpu.roll(low, 4, 0), block)


def cotangent_kernel(
    ids, rank_hbm, obs_hbm, area_hbm, vw_hbm, x_hbm, w_in_hbm, b_in_hbm, w_out_hbm, b_out_hbm,
    weight_ref, bout_ref, send0, send2, send1, send3, x_ref, w_in_ref, b_in_ref, w_out_ref, b_out_ref,
    every, rank_ref, obs_ref, area_ref, vw_ref, sems,
):
    pairs = [(rank_hbm, rank_ref), (obs_hbm, obs_ref), (area_hbm, area_ref), (vw_hbm, vw_ref)]
    needed = len(pairs)
    pairs += [(w_out_hbm, w_out_ref), (b_in_hbm, b_in_ref), (b_out_hbm, b_out_ref)]
    first = w_in_hbm.at[:, 0 : w_in_ref.shape[1]]
    for source, target in ((x_hbm, x_ref), (first, w_in_ref)):
        piece = source.shape[0] // 4
        for i in range(4):
            rows = pl.ds(i * piece, piece)
            pairs.append((source.at[rows, :], target.at[rows, :]))
    fetches = [
        pltpu.make_async_copy(source, target, sems.at[i]) for i, (source, target) in enumerate(pairs)
    ]
    for fetch in fetches:
        fetch.start()
    for fetch in fetches[:needed]:
        fetch.wait()
    n_mem, sub, n_vars = rank_ref.shape
    mem_dev = n_mem // 4
    epsil = (1.0 - ALPHA) / n_mem
    row = lax.broadcasted_iota(jnp.int32, (sub, sub), 0)
    lane = lax.broadcasted_iota(jnp.int32, (sub, sub), 1)
    area = jnp.sum(jnp.where(row == lane, area_ref[...], 0.0), axis=1, keepdims=True)
    weight = area * vw_ref[...]
    weight_ref[...] = weight
    obs = obs_ref[...]
    total = jnp.zeros_like(weight)
    for member in range(n_mem):
        rank = rank_ref[member]
        sign = jnp.where(rank >= obs, 1.0, -1.0)
        centred = (2 * rank - n_mem + 1).astype(F32)
        cot = (weight * (sign - (1.0 - epsil) / (n_mem - 1) * centred)).astype(BF16)
        every[member // mem_dev, member % mem_dev] = cot
        total = total + cot.astype(F32)
    bout_ref[...] = jnp.sum(total, axis=0, keepdims=True)
    y = ids[0]
    for k, out in enumerate((send0, send1, send2, send3)):
        out[...] = every[y ^ k]
    for fetch in fetches[needed:]:
        fetch.wait()


def forward_kernel(
    ids, x_ref, w_first, w_in_hbm, b_in_ref, w_out_ref, b_out_ref,
    hidden_ref, slope_ref, send0, send2, send1, send3, values, w_ref, sem,
):
    step = pl.program_id(0)
    mem_dev, sub, _ = send0.shape
    cols = w_first.shape[1]
    fetch = pltpu.make_async_copy(w_in_hbm.at[:, cols : 2 * cols], w_ref, sem)

    def half(weights):
        pre = jnp.dot(x_ref[...], weights[...], preferred_element_type=F32) + b_in_ref[...]
        square = pre * pre
        t = jnp.tanh(pre * (GELU_C + (GELU_C * GELU_A) * square))
        upper = 0.5 + 0.5 * t
        hidden = (pre * upper).astype(BF16)
        hidden_ref[...] = hidden
        slope_ref[...] = upper + pre * (0.5 - 0.5 * (t * t)) * (
            GELU_C + (3.0 * GELU_A * GELU_C) * square
        )
        return lax.dot_general(
            hidden, w_out_ref[...], (((1,), (1,)), ((), ())), preferred_element_type=F32
        )

    @pl.when(step == 0)
    def _():
        fetch.start()
        values[...] = half(w_first) + b_out_ref[...]

    @pl.when(step == 1)
    def _():
        fetch.wait()
        values[...] += half(w_ref)

    @pl.when(step == pl.num_programs(0) - 1)
    def _():
        y = ids[0]
        for k, out in enumerate((send0, send1, send2, send3)):
            dest = y ^ k
            for m in range(mem_dev):
                start = pl.multiple_of(m * 4 * sub + dest * sub, sub)
                out[m] = values[pl.ds(start, sub), :].astype(BF16)


def loss_kernel(got0, got2, got1, got3, target_ref, weight_ref, loss_ref):
    gots = (got0, got1, got2, got3)
    mem_dev = got0.shape[0]
    n_mem = 4 * mem_dev
    epsil = (1.0 - ALPHA) / n_mem
    ens = [got[m].astype(F32) for got in gots for m in range(mem_dev)]
    truth = target_ref[...]
    skill = jnp.zeros_like(truth)
    spread = jnp.zeros_like(truth)
    for j in range(n_mem):
        skill = skill + jnp.abs(ens[j] - truth)
        for k in range(j):
            spread = spread + jnp.abs(ens[j] - ens[k])
    cell = weight_ref[...] * (skill / n_mem - (1.0 - epsil) / (n_mem * (n_mem - 1)) * spread)
    loss_ref[...] = jnp.zeros((8, 128), F32) + jnp.sum(cell)


def backward_kernel(
    ids, got0, got2, got1, got3, x_ref, hidden_ref, slope_ref, w_out_ref, bout_ref,
    keep_ref, send_ref, back, back_wide, small,
):
    mem_dev, sub, n_vars = got0.shape
    core = ids[2]
    hid = hidden_ref.shape[1]
    y = ids[0]
    for k, got in enumerate((got0, got1, got2, got3)):
        source = y ^ k
        for m in range(mem_dev):
            start = pl.multiple_of(m * 4 * sub + source * sub, sub)
            back[pl.ds(start, sub), :] = got[m]
    var = lax.broadcasted_iota(jnp.int32, (n_vars, 128), 0)
    lane = lax.broadcasted_iota(jnp.int32, (n_vars, 128), 1)
    place = jnp.where(lane == var + 3 * (var // PER_BLOCK), 1.0, 0.0).astype(BF16)
    back_wide[...] = jnp.dot(back[...], place, preferred_element_type=F32).astype(BF16)

    for start in range(0, hid, 256):
        cols = slice(start, start + 256)
        upward = jnp.dot(back[...], w_out_ref[:, cols], preferred_element_type=F32)
        dhidden = (upward * slope_ref[:, cols]).astype(BF16)
        small[:, cols] = lax.dot_general(
            back_wide[...], hidden_ref[:, cols], (((0,), (0,)), ((), ())), preferred_element_type=F32
        )
        small[ROW_BIN : ROW_BIN + 1, cols] = jnp.sum(dhidden.astype(F32), axis=0, keepdims=True)
        grad = lax.dot_general(
            x_ref[...], dhidden, (((0,), (0,)), ((), ())), preferred_element_type=F32
        )
        grad = grad.reshape(32, 2, 16, 256)
        first, second = grad[:, 0], grad[:, 1]
        keep_ref[:, :, cols] = jnp.where(core == 0, first, second)
        send_ref[:, :, cols] = jnp.where(core == 0, second, first).astype(BF16)

    small[ROW_BOUT : ROW_BOUT + 1, 0:n_vars] = bout_ref[...]
    half = hid // 2
    mine = pl.ds(pl.multiple_of(core * half, half), half)
    other = pl.ds(pl.multiple_of((1 - core) * half, half), half)
    for q in range(8):
        rows = small[16 * q : 16 * q + 16, mine]
        for t in range(4):
            keep_ref[4 * q + t, :, hid:] = rows[:, t * 128 : (t + 1) * 128]
        rows = unfold(small[16 * q : 16 * q + 16, other]).astype(BF16)
        for t in range(4):
            send_ref[4 * q + t, :, hid:] = rows[:, t * 128 : (t + 1) * 128]


def payload_kernel(keep_ref, got_ref, out_hbm, out_ref, sems):
    n_plane, _, width = keep_ref.shape
    hid = width - 128
    piece = n_plane // 4
    stores = []
    for i in range(4):
        part = slice(i * piece, (i + 1) * piece)
        total = keep_ref[part, :, 0:hid] + got_ref[part, :, 0:hid].astype(F32)
        out_ref[part, :, 0:hid] = total.astype(BF16)
        for j in range(i * piece, (i + 1) * piece):
            block = unfold(keep_ref[j, :, hid:] + fold(got_ref[j, :, hid:].astype(F32)))
            out_ref[j, :, hid:] = block.astype(BF16)
        part = pl.ds(i * piece, piece)
        store = pltpu.make_async_copy(out_ref.at[part], out_hbm.at[part], sems.at[i])
        store.start()
        stores.append(store)
    for store in stores:
        store.wait()


def plane_kernel(ids, landed_ref, own_ref, small_ref, part2, part1, part3):
    hid = own_ref.shape[1]
    total = jnp.sum(landed_ref[...].astype(F32), axis=0)
    small = fold(total[:, hid:])
    small_ref[...] = small
    zhi = ids[1]
    quarters = [total[4 * z : 4 * z + 4, 0:hid] for z in range(4)]

    def quarter(which):
        out = quarters[3]
        for z in range(3):
            out = jnp.where(which == z, quarters[z], out)
        return out

    own_ref[...] = quarter(zhi)
    for k, out in ((1, part1), (2, part2), (3, part3)):
        rows = quarter(lax.rem(zhi + k, 4))
        for j in range(4):
            out[4 * j : 4 * j + 4, 0:256] = rows[:, j * 256 : (j + 1) * 256]
        out[:, 256:384] = small


def total_kernel(ids, own_ref, small_ref, got2, got1, got3, loss_ref, grad_ref, copies_ref):
    zhi = ids[1]
    for j in range(4):
        acc = own_ref[:, j * 256 : (j + 1) * 256]
        for got in (got1, got2, got3):
            acc = acc + got[4 * j : 4 * j + 4, 0:256]
        grad_ref[:, j * 256 : (j + 1) * 256] = acc
    parts = [small_ref[...]] + [got[:, 256:384] for got in (got1, got2, got3)]
    acc = None
    for source in range(4):
        term = parts[0]
        for k in range(1, 4):
            term = jnp.where(lax.rem(zhi + 4 - k, 4) == source, parts[k], term)
        acc = term if acc is None else acc + term
    row = lax.broadcasted_iota(jnp.int32, acc.shape, 0)
    acc = jnp.where(row == ROW_LOSS, loss_ref[0:1, :], acc)
    copies_ref[...] = jnp.broadcast_to(acc[None], copies_ref.shape)


def small_half(blocks, full):
    for q in range(8):
        for t in range(4):
            full[16 * q : 16 * q + 16, t * 128 : (t + 1) * 128] = blocks[4 * q + t]


def plain_rows(full, out_ref, scale):
    n_vars = out_ref.shape[0]
    for q in range(8):
        count = min(PER_BLOCK, n_vars - PER_BLOCK * q)
        out_ref[PER_BLOCK * q : PER_BLOCK * q + count, :] = full[16 * q : 16 * q + count, :] * scale


def own_kernel(
    scale, ids, grad_ref, mine, in_hbm, out_hbm, bin_hbm, full, in_ref, out_ref, bin_ref, sems
):
    half = full.shape[1]
    cols = pl.ds(pl.multiple_of(ids[2] * half, half), half)
    in_ref[...] = grad_ref[...] * scale
    small_half(mine, full)
    plain_rows(full, out_ref, scale)
    bin_ref[...] = full[ROW_BIN : ROW_BIN + 1, :] * scale
    stores = [
        pltpu.make_async_copy(out_ref, out_hbm.at[:, cols], sems.at[0]),
        pltpu.make_async_copy(in_ref, in_hbm, sems.at[1]),
        pltpu.make_async_copy(bin_ref, bin_hbm.at[:, cols], sems.at[2]),
    ]
    for copy in stores:
        copy.start()
    for copy in stores:
        copy.wait()


def other_kernel(
    scale, loss_scale, ids, out_before, bin_before, mine, theirs,
    out_hbm, bin_hbm, bout_hbm, loss_hbm, full, out_ref, bin_ref, bout_ref, loss_ref, sems,
):
    core = ids[2]
    half = full.shape[1]
    n_vars = out_ref.shape[0]
    cols = pl.ds(pl.multiple_of((1 - core) * half, half), half)
    small_half(theirs, full)
    plain_rows(full, out_ref, scale)
    bin_ref[...] = full[ROW_BIN : ROW_BIN + 1, :] * scale
    row = ROW_BOUT - 112
    here, there = mine[28, row : row + 1, :], theirs[28, row : row + 1, :]
    bout_ref[...] = jnp.where(core == 0, here, there)[:, 0:n_vars] * scale
    totals = []
    for blocks in (mine, theirs):
        total = jnp.zeros((1, 128), F32)
        for n in range(blocks.shape[0]):
            total = total + blocks[n, ROW_LOSS : ROW_LOSS + 1, :]
        totals.append(total)
    loss_ref[...] = (totals[0] + totals[1])[:, 0:1] * loss_scale
    stores = [
        pltpu.make_async_copy(out_ref, out_hbm.at[:, cols], sems.at[0]),
        pltpu.make_async_copy(bin_ref, bin_hbm.at[:, cols], sems.at[1]),
        pltpu.make_async_copy(bout_ref, bout_hbm, sems.at[2]),
        pltpu.make_async_copy(loss_ref, loss_hbm, sems.at[3]),
    ]
    for copy in stores:
        copy.start()
    for copy in stores:
        copy.wait()


def per_device(latents, w_in, b_in, w_out, b_out, targets, area, var_weight, member_rank, obs_rank):
    mem_dev = latents.shape[1]
    pts_dev = latents.shape[2]
    width = latents.shape[3]
    hid = w_in.shape[1]
    n_vars = w_out.shape[1]
    n_y = lax.axis_size("y")
    n_mem = mem_dev * n_y
    sub = pts_dev // n_y
    rows = mem_dev * pts_dev
    n_points = pts_dev * lax.axis_size(GRID)
    scale = 1.0 / math.sqrt(lax.axis_size("zhi") * n_mem * n_points)
    ids = jnp.stack(
        [lax.axis_index("y"), lax.axis_index("zhi"), lax.axis_index("core")]
    ).astype(jnp.int32)
    shape = jax.ShapeDtypeStruct

    x = latents.reshape(rows, width)
    w_out_t = w_out.T
    ranks = member_rank[0].transpose(0, 2, 1)
    obs = obs_rank[0].T
    truth = targets[0].T
    sent = shape((mem_dev, sub, n_vars), BF16)
    whole = pl.BlockSpec(memory_space=pltpu.VMEM)

    hbm = pl.BlockSpec(memory_space=pltpu.HBM)
    operands = [
        pltpu.with_memory_space_constraint(arr, pltpu.HBM)
        for arr in (
            ranks, obs, area[None, :], var_weight[None, :],
            x, w_in, b_in[None, :], w_out_t, b_out[None, :],
        )
    ]
    weight, bout, cot0, cot2, cot1, cot3, x, w_first, b_in, w_out_t, b_out = pl.pallas_call(
        cotangent_kernel,
        in_specs=[SMEM] + [hbm] * 9,
        out_specs=[whole] * 11,
        out_shape=[shape((sub, n_vars), F32), shape((1, n_vars), F32)]
        + [sent] * 4
        + [
            shape((rows, width), BF16),
            shape((width, hid // 2), BF16),
            shape((1, hid), F32),
            shape((n_vars, hid), BF16),
            shape((1, n_vars), F32),
        ],
        scratch_shapes=[
            pltpu.VMEM((n_y, mem_dev, sub, n_vars), BF16),
            pltpu.VMEM((n_mem, sub, n_vars), jnp.int32),
            pltpu.VMEM((sub, n_vars), jnp.int32),
            pltpu.VMEM((1, sub), F32),
            pltpu.VMEM((1, n_vars), F32),
            pltpu.SemaphoreType.DMA((15,)),
        ],
        compiler_params=PARAMS,
        name="cotangent",
    )(ids, *operands)
    ids_later, cot2, cot1, cot3 = lax.optimization_barrier((ids, cot2, cot1, cot3))
    cot2 = lax.ppermute(cot2, "y", pairs_of("y", 2))
    cot1 = lax.ppermute(cot1, "y", pairs_of("y", 1))
    cot3 = lax.ppermute(cot3, "y", pairs_of("y", 3))

    cols = hid // 2
    by_cols = lambda height: pl.BlockSpec((height, cols), lambda i: (0, i))
    hidden, slope, val0, val2, val1, val3 = pl.pallas_call(
        forward_kernel,
        grid=(hid // cols,),
        in_specs=[
            SMEM,
            const_spec((rows, width)),
            const_spec((width, cols)),
            hbm,
            by_cols(1),
            by_cols(n_vars),
            const_spec((1, n_vars)),
        ],
        out_specs=[by_cols(rows), by_cols(rows)] + [const_spec(sent.shape)] * 4,
        out_shape=[shape((rows, hid), BF16), shape((rows, hid), F32)] + [sent] * 4,
        scratch_shapes=[
            pltpu.VMEM((rows, n_vars), F32),
            pltpu.VMEM((width, cols), BF16),
            pltpu.SemaphoreType.DMA,
        ],
        compiler_params=PARAMS,
        name="forward",
    )(ids_later, x, w_first, operands[5], b_in, w_out_t, b_out)

    n_plane = lax.axis_size(PLANE)
    block = width // (2 * n_plane)
    keep, send = pl.pallas_call(
        backward_kernel,
        in_specs=[SMEM] + [whole] * 9,
        out_specs=[whole] * 2,
        out_shape=[
            shape((n_plane, block, hid + 128), F32),
            shape((n_plane, block, hid + 128), BF16),
        ],
        scratch_shapes=[
            pltpu.VMEM((rows, n_vars), BF16),
            pltpu.VMEM((rows, 128), BF16),
            pltpu.VMEM((128, hid), F32),
        ],
        compiler_params=PARAMS,
        name="backward",
    )(ids, cot0, cot2, cot1, cot3, x, hidden, slope, w_out_t, bout)

    swap = [(0, 1), (1, 0)]
    got = lax.ppermute(send, "core", swap)
    payload_shape = (n_plane, block, hid + 128)
    payload = pl.pallas_call(
        payload_kernel,
        in_specs=[whole] * 2,
        out_specs=hbm,
        out_shape=shape(payload_shape, BF16),
        scratch_shapes=[pltpu.VMEM(payload_shape, BF16), pltpu.SemaphoreType.DMA((4,))],
        compiler_params=PARAMS,
        name="payload",
    )(keep, got)
    payload, val2, val1, val3 = lax.optimization_barrier((payload, val2, val1, val3))
    landed = lax.all_to_all(payload, PLANE, 0, 0, tiled=True)
    val2 = lax.ppermute(val2, "y", pairs_of("y", 2))
    val1 = lax.ppermute(val1, "y", pairs_of("y", 1))
    val3 = lax.ppermute(val3, "y", pairs_of("y", 3))
    part_loss = pl.pallas_call(
        loss_kernel,
        in_specs=[whole] * 6,
        out_specs=whole,
        out_shape=shape((8, 128), F32),
        compiler_params=PARAMS,
        name="loss",
    )(val0, val2, val1, val3, truth, weight)

    part = shape((block, 384), F32)
    own, small, part2, part1, part3 = pl.pallas_call(
        plane_kernel,
        in_specs=[SMEM, whole],
        out_specs=[whole] * 5,
        out_shape=[shape((block // 4, hid), F32), shape((block, 128), F32), part, part, part],
        compiler_params=PARAMS,
        name="plane_sum",
    )(ids, landed)
    part2 = lax.ppermute(part2, "zhi", shift("zhi", 2))
    part1 = lax.ppermute(part1, "zhi", shift("zhi", 1))
    part3 = lax.ppermute(part3, "zhi", shift("zhi", 3))
    grad_in, copies = pl.pallas_call(
        total_kernel,
        in_specs=[SMEM] + [whole] * 6,
        out_specs=[whole] * 2,
        out_shape=[shape((block // 4, hid), F32), shape((n_plane, block, 128), F32)],
        compiler_params=PARAMS,
        name="total",
    )(ids, own, small, part2, part1, part3, part_loss)

    mine = lax.all_to_all(copies, PLANE, 0, 0, tiled=True)
    theirs = lax.ppermute(mine, "core", swap)
    half = hid // 2
    in_shape = shape((block // 4, hid), F32)
    out_shape = shape((n_vars, hid), F32)
    bin_shape = shape((1, hid), F32)
    bout_shape = shape((1, n_vars), F32)
    loss_shape = shape((1, 1), F32)
    grad_in, grad_out, grad_bin = pl.pallas_call(
        lambda *refs: own_kernel(scale, *refs),
        in_specs=[SMEM] + [whole] * 2,
        out_specs=[hbm] * 3,
        out_shape=[in_shape, out_shape, bin_shape],
        scratch_shapes=[
            pltpu.VMEM((128, half), F32),
            pltpu.VMEM(in_shape.shape, F32),
            pltpu.VMEM((n_vars, half), F32),
            pltpu.VMEM((1, half), F32),
            pltpu.SemaphoreType.DMA((3,)),
        ],
        compiler_params=PARAMS,
        name="unpack_own",
    )(ids, grad_in, mine)
    grad_out, grad_bin, grad_bout, loss = pl.pallas_call(
        lambda *refs: other_kernel(scale, 1.0 / (n_points * n_vars), *refs),
        in_specs=[SMEM, hbm, hbm] + [whole] * 2,
        out_specs=[hbm] * 4,
        out_shape=[out_shape, bin_shape, bout_shape, loss_shape],
        input_output_aliases={1: 0, 2: 1},
        scratch_shapes=[
            pltpu.VMEM((128, half), F32),
            pltpu.VMEM((n_vars, half), F32),
            pltpu.VMEM((1, half), F32),
            pltpu.VMEM(bout_shape.shape, F32),
            pltpu.VMEM(loss_shape.shape, F32),
            pltpu.SemaphoreType.DMA((4,)),
        ],
        compiler_params=PARAMS,
        name="unpack_other",
    )(ids, grad_out, grad_bin, mine, theirs)
    return (loss.reshape(1), grad_in, grad_out.T, grad_bin.reshape(hid), grad_bout.reshape(n_vars))


def solution(mesh):
    split = Mesh(mesh.devices.reshape(4, 2, 4, 2, 4), NAMES)
    points = GRID + ("y",)
    in_specs = (
        P("zhi", "y", GRID, None),
        P(),
        P(),
        P(),
        P(),
        P("zhi", None, points),
        P(points),
        P(),
        P("zhi", None, None, points),
        P("zhi", None, points),
    )
    out_specs = (P("zhi"), P(NAMES, None), P(), P(), P())
    return jax.shard_map(
        per_device, mesh=split, in_specs=in_specs, out_specs=out_specs, check_vma=False
    )
```

```python
import math

import jax
import jax.numpy as jnp
from jax import lax
from jax.experimental import pallas as pl
from jax.experimental.pallas import tpu as pltpu
from jax.sharding import Mesh
from jax.sharding import PartitionSpec as P

ALPHA = 0.95
NAMES = ("y", "zlo", "x", "core", "zhi")
PLANE = ("y", "zlo", "x")
GRID = ("zlo", "x", "core")
F32 = jnp.float32
BF16 = jnp.bfloat16
GELU_C = math.sqrt(2.0 / math.pi)
GELU_A = 0.044715
PARAMS = pltpu.CompilerParams(vmem_limit_bytes=24 * 1024 * 1024)
SMEM = pl.BlockSpec(memory_space=pltpu.SMEM)

PER_BLOCK = 13
ROW_BIN, ROW_BOUT, ROW_LOSS = 121, 122, 15


def shift(axis, step):
    size = lax.axis_size(axis)
    return [(i, (i + step) % size) for i in range(size)]


def pairs_of(axis, step):
    return [(i, i ^ step) for i in range(lax.axis_size(axis))]


def const_spec(shape):
    return pl.BlockSpec(shape, lambda *_: (0,) * len(shape))


def fold(block):
    row = lax.broadcasted_iota(jnp.int32, block.shape, 0)
    up = pltpu.roll(block, 12, 0)
    low = (row == 13) | (row == 14)
    return jnp.where((row == 9) | (row == 10), block + up, jnp.where(low, 0.0, block))


def unfold(block):
    row = lax.broadcasted_iota(jnp.int32, block.shape, 0)
    low = block - block.astype(BF16).astype(F32)
    return jnp.where((row == 13) | (row == 14), pltpu.roll(low, 4, 0), block)


def cotangent_kernel(
    ids, rank_hbm, obs_hbm, area_hbm, vw_hbm, x_hbm, w_in_hbm, b_in_hbm, b_out_hbm,
    weight_ref, bout_ref, send0, send2, send1, send3, x_ref, w_in_ref, b_in_ref, b_out_ref,
    every, rank_ref, obs_ref, area_ref, vw_ref, sems,
):
    pairs = [(rank_hbm, rank_ref), (obs_hbm, obs_ref), (area_hbm, area_ref), (vw_hbm, vw_ref)]
    needed = len(pairs)
    pairs += [(b_in_hbm, b_in_ref), (b_out_hbm, b_out_ref)]
    first = w_in_hbm.at[:, 0 : w_in_ref.shape[1]]
    for source, target in ((x_hbm, x_ref), (first, w_in_ref)):
        piece = source.shape[0] // 4
        for i in range(4):
            rows = pl.ds(i * piece, piece)
            pairs.append((source.at[rows, :], target.at[rows, :]))
    fetches = [
        pltpu.make_async_copy(source, target, sems.at[i]) for i, (source, target) in enumerate(pairs)
    ]
    for fetch in fetches:
        fetch.start()
    for fetch in fetches[:needed]:
        fetch.wait()
    n_mem, sub, n_vars = rank_ref.shape
    mem_dev = n_mem // 4
    epsil = (1.0 - ALPHA) / n_mem
    row = lax.broadcasted_iota(jnp.int32, (sub, sub), 0)
    lane = lax.broadcasted_iota(jnp.int32, (sub, sub), 1)
    area = jnp.sum(jnp.where(row == lane, area_ref[...], 0.0), axis=1, keepdims=True)
    weight = area * vw_ref[...]
    weight_ref[...] = weight
    obs = obs_ref[...]
    total = jnp.zeros_like(weight)
    for member in range(n_mem):
        rank = rank_ref[member]
        sign = jnp.where(rank >= obs, 1.0, -1.0)
        centred = (2 * rank - n_mem + 1).astype(F32)
        cot = (weight * (sign - (1.0 - epsil) / (n_mem - 1) * centred)).astype(BF16)
        every[member // mem_dev, member % mem_dev] = cot
        total = total + cot.astype(F32)
    bout_ref[...] = jnp.sum(total, axis=0, keepdims=True)
    y = ids[0]
    for k, out in enumerate((send0, send1, send2, send3)):
        out[...] = every[y ^ k]
    for fetch in fetches[needed:]:
        fetch.wait()


def forward_kernel(
    ids, x_ref, w_first, w_in_hbm, b_in_ref, w_out_ref, b_out_ref,
    hidden_ref, slope_ref, w_out_copy, send0, send2, send1, send3, values, w_ref, sem,
):
    step = pl.program_id(0)
    mem_dev, sub, _ = send0.shape
    cols = w_first.shape[1]
    w_out_copy[...] = w_out_ref[...]
    fetch = pltpu.make_async_copy(w_in_hbm.at[:, cols : 2 * cols], w_ref, sem)

    def half(weights):
        pre = jnp.dot(x_ref[...], weights[...], preferred_element_type=F32) + b_in_ref[...]
        square = pre * pre
        t = jnp.tanh(pre * (GELU_C + (GELU_C * GELU_A) * square))
        upper = 0.5 + 0.5 * t
        hidden = (pre * upper).astype(BF16)
        hidden_ref[...] = hidden
        slope_ref[...] = upper + pre * (0.5 - 0.5 * (t * t)) * (
            GELU_C + (3.0 * GELU_A * GELU_C) * square
        )
        return lax.dot_general(
            hidden, w_out_ref[...], (((1,), (1,)), ((), ())), preferred_element_type=F32
        )

    @pl.when(step == 0)
    def _():
        fetch.start()
        values[...] = half(w_first) + b_out_ref[...]

    @pl.when(step == 1)
    def _():
        fetch.wait()
        values[...] += half(w_ref)

    @pl.when(step == pl.num_programs(0) - 1)
    def _():
        y = ids[0]
        for k, out in enumerate((send0, send1, send2, send3)):
            dest = y ^ k
            for m in range(mem_dev):
                start = pl.multiple_of(m * 4 * sub + dest * sub, sub)
                out[m] = values[pl.ds(start, sub), :].astype(BF16)


def loss_kernel(got0, got2, got1, got3, target_ref, weight_ref, loss_ref):
    gots = (got0, got1, got2, got3)
    mem_dev = got0.shape[0]
    n_mem = 4 * mem_dev
    epsil = (1.0 - ALPHA) / n_mem
    ens = [got[m].astype(F32) for got in gots for m in range(mem_dev)]
    truth = target_ref[...]
    skill = jnp.zeros_like(truth)
    spread = jnp.zeros_like(truth)
    for j in range(n_mem):
        skill = skill + jnp.abs(ens[j] - truth)
        for k in range(j):
            spread = spread + jnp.abs(ens[j] - ens[k])
    cell = weight_ref[...] * (skill / n_mem - (1.0 - epsil) / (n_mem * (n_mem - 1)) * spread)
    loss_ref[...] = jnp.zeros((8, 128), F32) + jnp.sum(cell)


def backward_kernel(
    ids, got0, got2, got1, got3, x_ref, hidden_ref, slope_ref, w_out_ref, bout_ref,
    keep_ref, send_ref, back, back_wide, small,
):
    mem_dev, sub, n_vars = got0.shape
    core = ids[2]
    hid = hidden_ref.shape[1]
    y = ids[0]
    for k, got in enumerate((got0, got1, got2, got3)):
        source = y ^ k
        for m in range(mem_dev):
            start = pl.multiple_of(m * 4 * sub + source * sub, sub)
            back[pl.ds(start, sub), :] = got[m]
    var = lax.broadcasted_iota(jnp.int32, (n_vars, 128), 0)
    lane = lax.broadcasted_iota(jnp.int32, (n_vars, 128), 1)
    place = jnp.where(lane == var + 3 * (var // PER_BLOCK), 1.0, 0.0).astype(BF16)
    back_wide[...] = jnp.dot(back[...], place, preferred_element_type=F32).astype(BF16)

    for start in range(0, hid, 256):
        cols = slice(start, start + 256)
        upward = jnp.dot(back[...], w_out_ref[:, cols], preferred_element_type=F32)
        dhidden = (upward * slope_ref[:, cols]).astype(BF16)
        small[:, cols] = lax.dot_general(
            back_wide[...], hidden_ref[:, cols], (((0,), (0,)), ((), ())), preferred_element_type=F32
        )
        small[ROW_BIN : ROW_BIN + 1, cols] = jnp.sum(dhidden.astype(F32), axis=0, keepdims=True)
        grad = lax.dot_general(
            x_ref[...], dhidden, (((0,), (0,)), ((), ())), preferred_element_type=F32
        )
        grad = grad.reshape(32, 2, 16, 256)
        first, second = grad[:, 0], grad[:, 1]
        keep_ref[:, :, cols] = jnp.where(core == 0, first, second)
        send_ref[:, :, cols] = jnp.where(core == 0, second, first).astype(BF16)

    small[ROW_BOUT : ROW_BOUT + 1, 0:n_vars] = bout_ref[...]
    half = hid // 2
    mine = pl.ds(pl.multiple_of(core * half, half), half)
    other = pl.ds(pl.multiple_of((1 - core) * half, half), half)
    for q in range(8):
        rows = small[16 * q : 16 * q + 16, mine]
        for t in range(4):
            keep_ref[4 * q + t, :, hid:] = rows[:, t * 128 : (t + 1) * 128]
        rows = unfold(small[16 * q : 16 * q + 16, other]).astype(BF16)
        for t in range(4):
            send_ref[4 * q + t, :, hid:] = rows[:, t * 128 : (t + 1) * 128]


def payload_kernel(keep_ref, got_ref, out_hbm, out_ref, sems):
    n_plane, _, width = keep_ref.shape
    hid = width - 128
    piece = n_plane // 4
    stores = []
    for i in range(4):
        part = slice(i * piece, (i + 1) * piece)
        total = keep_ref[part, :, 0:hid] + got_ref[part, :, 0:hid].astype(F32)
        out_ref[part, :, 0:hid] = total.astype(BF16)
        for j in range(i * piece, (i + 1) * piece):
            block = unfold(keep_ref[j, :, hid:] + fold(got_ref[j, :, hid:].astype(F32)))
            out_ref[j, :, hid:] = block.astype(BF16)
        part = pl.ds(i * piece, piece)
        store = pltpu.make_async_copy(out_ref.at[part], out_hbm.at[part], sems.at[i])
        store.start()
        stores.append(store)
    for store in stores:
        store.wait()


def plane_kernel(ids, landed_ref, own_ref, small_ref, part2, part1, part3):
    hid = own_ref.shape[1]
    total = jnp.sum(landed_ref[...].astype(F32), axis=0)
    small = fold(total[:, hid:])
    small_ref[...] = small
    zhi = ids[1]
    quarters = [total[4 * z : 4 * z + 4, 0:hid] for z in range(4)]

    def quarter(which):
        out = quarters[3]
        for z in range(3):
            out = jnp.where(which == z, quarters[z], out)
        return out

    own_ref[...] = quarter(zhi)
    for k, out in ((1, part1), (2, part2), (3, part3)):
        rows = quarter(lax.rem(zhi + k, 4))
        for j in range(4):
            out[4 * j : 4 * j + 4, 0:256] = rows[:, j * 256 : (j + 1) * 256]
        out[:, 256:384] = small


def total_kernel(ids, own_ref, small_ref, got2, got1, got3, loss_ref, grad_ref, copies_ref):
    zhi = ids[1]
    for j in range(4):
        acc = own_ref[:, j * 256 : (j + 1) * 256]
        for got in (got1, got2, got3):
            acc = acc + got[4 * j : 4 * j + 4, 0:256]
        grad_ref[:, j * 256 : (j + 1) * 256] = acc
    parts = [small_ref[...]] + [got[:, 256:384] for got in (got1, got2, got3)]
    acc = None
    for source in range(4):
        term = parts[0]
        for k in range(1, 4):
            term = jnp.where(lax.rem(zhi + 4 - k, 4) == source, parts[k], term)
        acc = term if acc is None else acc + term
    row = lax.broadcasted_iota(jnp.int32, acc.shape, 0)
    acc = jnp.where(row == ROW_LOSS, loss_ref[0:1, :], acc)
    copies_ref[...] = jnp.broadcast_to(acc[None], copies_ref.shape)


def small_half(blocks, full):
    for q in range(8):
        for t in range(4):
            full[16 * q : 16 * q + 16, t * 128 : (t + 1) * 128] = blocks[4 * q + t]


def plain_rows(full, out_ref, scale):
    n_vars = out_ref.shape[0]
    for q in range(8):
        count = min(PER_BLOCK, n_vars - PER_BLOCK * q)
        out_ref[PER_BLOCK * q : PER_BLOCK * q + count, :] = full[16 * q : 16 * q + count, :] * scale


def own_kernel(
    scale, ids, grad_ref, mine, in_hbm, out_hbm, bin_hbm, full, in_ref, out_ref, bin_ref, sems
):
    half = full.shape[1]
    cols = pl.ds(pl.multiple_of(ids[2] * half, half), half)
    in_ref[...] = grad_ref[...] * scale
    small_half(mine, full)
    plain_rows(full, out_ref, scale)
    bin_ref[...] = full[ROW_BIN : ROW_BIN + 1, :] * scale
    stores = [
        pltpu.make_async_copy(out_ref, out_hbm.at[:, cols], sems.at[0]),
        pltpu.make_async_copy(in_ref, in_hbm, sems.at[1]),
        pltpu.make_async_copy(bin_ref, bin_hbm.at[:, cols], sems.at[2]),
    ]
    for copy in stores:
        copy.start()
    for copy in stores:
        copy.wait()


def other_kernel(
    scale, loss_scale, ids, out_before, bin_before, mine, theirs,
    out_hbm, bin_hbm, bout_hbm, loss_hbm, full, out_ref, bin_ref, bout_ref, loss_ref, sems,
):
    core = ids[2]
    half = full.shape[1]
    n_vars = out_ref.shape[0]
    cols = pl.ds(pl.multiple_of((1 - core) * half, half), half)
    small_half(theirs, full)
    plain_rows(full, out_ref, scale)
    bin_ref[...] = full[ROW_BIN : ROW_BIN + 1, :] * scale
    row = ROW_BOUT - 112
    here, there = mine[28, row : row + 1, :], theirs[28, row : row + 1, :]
    bout_ref[...] = jnp.where(core == 0, here, there)[:, 0:n_vars] * scale
    totals = []
    for blocks in (mine, theirs):
        total = jnp.zeros((1, 128), F32)
        for n in range(blocks.shape[0]):
            total = total + blocks[n, ROW_LOSS : ROW_LOSS + 1, :]
        totals.append(total)
    loss_ref[...] = (totals[0] + totals[1])[:, 0:1] * loss_scale
    stores = [
        pltpu.make_async_copy(out_ref, out_hbm.at[:, cols], sems.at[0]),
        pltpu.make_async_copy(bin_ref, bin_hbm.at[:, cols], sems.at[1]),
        pltpu.make_async_copy(bout_ref, bout_hbm, sems.at[2]),
        pltpu.make_async_copy(loss_ref, loss_hbm, sems.at[3]),
    ]
    for copy in stores:
        copy.start()
    for copy in stores:
        copy.wait()


def per_device(latents, w_in, b_in, w_out, b_out, targets, area, var_weight, member_rank, obs_rank):
    mem_dev = latents.shape[1]
    pts_dev = latents.shape[2]
    width = latents.shape[3]
    hid = w_in.shape[1]
    n_vars = w_out.shape[1]
    n_y = lax.axis_size("y")
    n_mem = mem_dev * n_y
    sub = pts_dev // n_y
    rows = mem_dev * pts_dev
    n_points = pts_dev * lax.axis_size(GRID)
    scale = 1.0 / math.sqrt(lax.axis_size("zhi") * n_mem * n_points)
    ids = jnp.stack(
        [lax.axis_index("y"), lax.axis_index("zhi"), lax.axis_index("core")]
    ).astype(jnp.int32)
    shape = jax.ShapeDtypeStruct

    x = latents.reshape(rows, width)
    w_out_t = w_out.T
    ranks = member_rank[0].transpose(0, 2, 1)
    obs = obs_rank[0].T
    truth = targets[0].T
    sent = shape((mem_dev, sub, n_vars), BF16)
    whole = pl.BlockSpec(memory_space=pltpu.VMEM)

    hbm = pl.BlockSpec(memory_space=pltpu.HBM)
    operands = [
        pltpu.with_memory_space_constraint(arr, pltpu.HBM)
        for arr in (
            ranks, obs, area[None, :], var_weight[None, :],
            x, w_in, b_in[None, :], b_out[None, :], w_out_t,
        )
    ]
    w_in_hbm, w_out_hbm = operands[5], operands[8]
    weight, bout, cot0, cot2, cot1, cot3, x, w_first, b_in, b_out = pl.pallas_call(
        cotangent_kernel,
        in_specs=[SMEM] + [hbm] * 8,
        out_specs=[whole] * 10,
        out_shape=[shape((sub, n_vars), F32), shape((1, n_vars), F32)]
        + [sent] * 4
        + [
            shape((rows, width), BF16),
            shape((width, hid // 2), BF16),
            shape((1, hid), F32),
            shape((1, n_vars), F32),
        ],
        scratch_shapes=[
            pltpu.VMEM((n_y, mem_dev, sub, n_vars), BF16),
            pltpu.VMEM((n_mem, sub, n_vars), jnp.int32),
            pltpu.VMEM((sub, n_vars), jnp.int32),
            pltpu.VMEM((1, sub), F32),
            pltpu.VMEM((1, n_vars), F32),
            pltpu.SemaphoreType.DMA((14,)),
        ],
        compiler_params=PARAMS,
        name="cotangent",
    )(ids, *operands[:8])
    ids_later, cot2, cot1, cot3 = lax.optimization_barrier((ids, cot2, cot1, cot3))
    cot2 = lax.ppermute(cot2, "y", pairs_of("y", 2))
    cot1 = lax.ppermute(cot1, "y", pairs_of("y", 1))
    cot3 = lax.ppermute(cot3, "y", pairs_of("y", 3))

    cols = hid // 2
    by_cols = lambda height: pl.BlockSpec((height, cols), lambda i: (0, i))
    hidden, slope, w_out_t, val0, val2, val1, val3 = pl.pallas_call(
        forward_kernel,
        grid=(hid // cols,),
        in_specs=[
            SMEM,
            const_spec((rows, width)),
            const_spec((width, cols)),
            hbm,
            by_cols(1),
            by_cols(n_vars),
            const_spec((1, n_vars)),
        ],
        out_specs=[by_cols(rows), by_cols(rows), by_cols(n_vars)] + [const_spec(sent.shape)] * 4,
        out_shape=[shape((rows, hid), BF16), shape((rows, hid), F32), shape((n_vars, hid), BF16)]
        + [sent] * 4,
        scratch_shapes=[
            pltpu.VMEM((rows, n_vars), F32),
            pltpu.VMEM((width, cols), BF16),
            pltpu.SemaphoreType.DMA,
        ],
        compiler_params=PARAMS,
        name="forward",
    )(ids_later, x, w_first, w_in_hbm, b_in, w_out_hbm, b_out)

    n_plane = lax.axis_size(PLANE)
    block = width // (2 * n_plane)
    keep, send = pl.pallas_call(
        backward_kernel,
        in_specs=[SMEM] + [whole] * 9,
        out_specs=[whole] * 2,
        out_shape=[
            shape((n_plane, block, hid + 128), F32),
            shape((n_plane, block, hid + 128), BF16),
        ],
        scratch_shapes=[
            pltpu.VMEM((rows, n_vars), BF16),
            pltpu.VMEM((rows, 128), BF16),
            pltpu.VMEM((128, hid), F32),
        ],
        compiler_params=PARAMS,
        name="backward",
    )(ids, cot0, cot2, cot1, cot3, x, hidden, slope, w_out_t, bout)

    swap = [(0, 1), (1, 0)]
    got = lax.ppermute(send, "core", swap)
    payload_shape = (n_plane, block, hid + 128)
    payload = pl.pallas_call(
        payload_kernel,
        in_specs=[whole] * 2,
        out_specs=hbm,
        out_shape=shape(payload_shape, BF16),
        scratch_shapes=[pltpu.VMEM(payload_shape, BF16), pltpu.SemaphoreType.DMA((4,))],
        compiler_params=PARAMS,
        name="payload",
    )(keep, got)
    payload, val2, val1, val3 = lax.optimization_barrier((payload, val2, val1, val3))
    landed = lax.all_to_all(payload, PLANE, 0, 0, tiled=True)
    val2 = lax.ppermute(val2, "y", pairs_of("y", 2))
    val1 = lax.ppermute(val1, "y", pairs_of("y", 1))
    val3 = lax.ppermute(val3, "y", pairs_of("y", 3))
    part_loss = pl.pallas_call(
        loss_kernel,
        in_specs=[whole] * 6,
        out_specs=whole,
        out_shape=shape((8, 128), F32),
        compiler_params=PARAMS,
        name="loss",
    )(val0, val2, val1, val3, truth, weight)

    part = shape((block, 384), F32)
    own, small, part2, part1, part3 = pl.pallas_call(
        plane_kernel,
        in_specs=[SMEM, whole],
        out_specs=[whole] * 5,
        out_shape=[shape((block // 4, hid), F32), shape((block, 128), F32), part, part, part],
        compiler_params=PARAMS,
        name="plane_sum",
    )(ids, landed)
    part2 = lax.ppermute(part2, "zhi", shift("zhi", 2))
    part1 = lax.ppermute(part1, "zhi", shift("zhi", 1))
    part3 = lax.ppermute(part3, "zhi", shift("zhi", 3))
    grad_in, copies = pl.pallas_call(
        total_kernel,
        in_specs=[SMEM] + [whole] * 6,
        out_specs=[whole] * 2,
        out_shape=[shape((block // 4, hid), F32), shape((n_plane, block, 128), F32)],
        compiler_params=PARAMS,
        name="total",
    )(ids, own, small, part2, part1, part3, part_loss)

    mine = lax.all_to_all(copies, PLANE, 0, 0, tiled=True)
    theirs = lax.ppermute(mine, "core", swap)
    half = hid // 2
    in_shape = shape((block // 4, hid), F32)
    out_shape = shape((n_vars, hid), F32)
    bin_shape = shape((1, hid), F32)
    bout_shape = shape((1, n_vars), F32)
    loss_shape = shape((1, 1), F32)
    grad_in, grad_out, grad_bin = pl.pallas_call(
        lambda *refs: own_kernel(scale, *refs),
        in_specs=[SMEM] + [whole] * 2,
        out_specs=[hbm] * 3,
        out_shape=[in_shape, out_shape, bin_shape],
        scratch_shapes=[
            pltpu.VMEM((128, half), F32),
            pltpu.VMEM(in_shape.shape, F32),
            pltpu.VMEM((n_vars, half), F32),
            pltpu.VMEM((1, half), F32),
            pltpu.SemaphoreType.DMA((3,)),
        ],
        compiler_params=PARAMS,
        name="unpack_own",
    )(ids, grad_in, mine)
    grad_out, grad_bin, grad_bout, loss = pl.pallas_call(
        lambda *refs: other_kernel(scale, 1.0 / (n_points * n_vars), *refs),
        in_specs=[SMEM, hbm, hbm] + [whole] * 2,
        out_specs=[hbm] * 4,
        out_shape=[out_shape, bin_shape, bout_shape, loss_shape],
        input_output_aliases={1: 0, 2: 1},
        scratch_shapes=[
            pltpu.VMEM((128, half), F32),
            pltpu.VMEM((n_vars, half), F32),
            pltpu.VMEM((1, half), F32),
            pltpu.VMEM(bout_shape.shape, F32),
            pltpu.VMEM(loss_shape.shape, F32),
            pltpu.SemaphoreType.DMA((4,)),
        ],
        compiler_params=PARAMS,
        name="unpack_other",
    )(ids, grad_out, grad_bin, mine, theirs)
    return (loss.reshape(1), grad_in, grad_out.T, grad_bin.reshape(hid), grad_bout.reshape(n_vars))


def solution(mesh):
    split = Mesh(mesh.devices.reshape(4, 2, 4, 2, 4), NAMES)
    points = GRID + ("y",)
    in_specs = (
        P("zhi", "y", GRID, None),
        P(),
        P(),
        P(),
        P(),
        P("zhi", None, points),
        P(points),
        P(),
        P("zhi", None, None, points),
        P("zhi", None, points),
    )
    out_specs = (P("zhi"), P(NAMES, None), P(), P(), P())
    return jax.shard_map(
        per_device, mesh=split, in_specs=in_specs, out_specs=out_specs, check_vma=False
    )
```

```python
import math

import jax
import jax.numpy as jnp
from jax import lax
from jax.experimental import pallas as pl
from jax.experimental.pallas import tpu as pltpu
from jax.sharding import Mesh
from jax.sharding import PartitionSpec as P

ALPHA = 0.95
NAMES = ("y", "zlo", "x", "core", "zhi")
PLANE = ("y", "zlo", "x")
GRID = ("zlo", "x", "core")
F32 = jnp.float32
BF16 = jnp.bfloat16
GELU_C = math.sqrt(2.0 / math.pi)
GELU_A = 0.044715
PARAMS = pltpu.CompilerParams(vmem_limit_bytes=24 * 1024 * 1024)
SMEM = pl.BlockSpec(memory_space=pltpu.SMEM)

PER_BLOCK = 13
ROW_BIN, ROW_BOUT, ROW_LOSS = 121, 122, 15


def shift(axis, step):
    size = lax.axis_size(axis)
    return [(i, (i + step) % size) for i in range(size)]


def pairs_of(axis, step):
    return [(i, i ^ step) for i in range(lax.axis_size(axis))]


def const_spec(shape):
    return pl.BlockSpec(shape, lambda *_: (0,) * len(shape))


def fold(block):
    row = lax.broadcasted_iota(jnp.int32, block.shape, 0)
    up = pltpu.roll(block, 12, 0)
    low = (row == 13) | (row == 14)
    return jnp.where((row == 9) | (row == 10), block + up, jnp.where(low, 0.0, block))


def unfold(block):
    row = lax.broadcasted_iota(jnp.int32, block.shape, 0)
    low = block - block.astype(BF16).astype(F32)
    return jnp.where((row == 13) | (row == 14), pltpu.roll(low, 4, 0), block)


def cotangent_kernel(
    ids, rank_hbm, obs_hbm, area_hbm, vw_hbm, x_hbm, w_in_hbm, b_in_hbm, b_out_hbm,
    weight_ref, bout_ref, send0, send2, send1, send3, x_ref, w_in_ref, b_in_ref, b_out_ref,
    every, rank_ref, obs_ref, area_ref, vw_ref, sems,
):
    pairs = [(rank_hbm, rank_ref), (obs_hbm, obs_ref), (area_hbm, area_ref), (vw_hbm, vw_ref)]
    needed = len(pairs)
    pairs += [(b_in_hbm, b_in_ref), (b_out_hbm, b_out_ref)]
    first = w_in_hbm.at[:, 0 : w_in_ref.shape[1]]
    for source, target in ((x_hbm, x_ref), (first, w_in_ref)):
        piece = source.shape[0] // 4
        for i in range(4):
            rows = pl.ds(i * piece, piece)
            pairs.append((source.at[rows, :], target.at[rows, :]))
    fetches = [
        pltpu.make_async_copy(source, target, sems.at[i]) for i, (source, target) in enumerate(pairs)
    ]
    for fetch in fetches:
        fetch.start()
    for fetch in fetches[:needed]:
        fetch.wait()
    n_mem, sub, n_vars = rank_ref.shape
    mem_dev = n_mem // 4
    epsil = (1.0 - ALPHA) / n_mem
    row = lax.broadcasted_iota(jnp.int32, (sub, sub), 0)
    lane = lax.broadcasted_iota(jnp.int32, (sub, sub), 1)
    area = jnp.sum(jnp.where(row == lane, area_ref[...], 0.0), axis=1, keepdims=True)
    weight = area * vw_ref[...]
    weight_ref[...] = weight
    obs = obs_ref[...]
    total = jnp.zeros_like(weight)
    for member in range(n_mem):
        rank = rank_ref[member]
        sign = jnp.where(rank >= obs, 1.0, -1.0)
        centred = (2 * rank - n_mem + 1).astype(F32)
        cot = (weight * (sign - (1.0 - epsil) / (n_mem - 1) * centred)).astype(BF16)
        every[member // mem_dev, member % mem_dev] = cot
        total = total + cot.astype(F32)
    bout_ref[...] = jnp.sum(total, axis=0, keepdims=True)
    y = ids[0]
    for k, out in enumerate((send0, send1, send2, send3)):
        out[...] = every[y ^ k]
    for fetch in fetches[needed:]:
        fetch.wait()


def forward_kernel(x_ref, w_first, w_in_hbm, b_in_ref, hidden_ref, slope_ref, w_ref, sem):
    step = pl.program_id(0)
    cols = w_first.shape[1]
    fetch = pltpu.make_async_copy(w_in_hbm.at[:, cols : 2 * cols], w_ref, sem)

    def half(weights):
        pre = jnp.dot(x_ref[...], weights[...], preferred_element_type=F32) + b_in_ref[...]
        square = pre * pre
        t = jnp.tanh(pre * (GELU_C + (GELU_C * GELU_A) * square))
        upper = 0.5 + 0.5 * t
        hidden_ref[...] = (pre * upper).astype(BF16)
        slope_ref[...] = upper + pre * (0.5 - 0.5 * (t * t)) * (
            GELU_C + (3.0 * GELU_A * GELU_C) * square
        )

    @pl.when(step == 0)
    def _():
        fetch.start()
        half(w_first)

    @pl.when(step == 1)
    def _():
        fetch.wait()
        half(w_ref)


def forecast_kernel(
    ids, hidden_ref, w_out_ref, b_out_ref, send0, send2, send1, send3, values
):
    mem_dev, sub, _ = send0.shape
    values[...] = b_out_ref[...] + lax.dot_general(
        hidden_ref[...], w_out_ref[...], (((1,), (1,)), ((), ())), preferred_element_type=F32
    )
    y = ids[0]
    for k, out in enumerate((send0, send1, send2, send3)):
        dest = y ^ k
        for m in range(mem_dev):
            start = pl.multiple_of(m * 4 * sub + dest * sub, sub)
            out[m] = values[pl.ds(start, sub), :].astype(BF16)


def loss_kernel(got0, got2, got1, got3, target_ref, weight_ref, loss_ref):
    gots = (got0, got1, got2, got3)
    mem_dev = got0.shape[0]
    n_mem = 4 * mem_dev
    epsil = (1.0 - ALPHA) / n_mem
    ens = [got[m].astype(F32) for got in gots for m in range(mem_dev)]
    truth = target_ref[...]
    skill = jnp.zeros_like(truth)
    spread = jnp.zeros_like(truth)
    for j in range(n_mem):
        skill = skill + jnp.abs(ens[j] - truth)
        for k in range(j):
            spread = spread + jnp.abs(ens[j] - ens[k])
    cell = weight_ref[...] * (skill / n_mem - (1.0 - epsil) / (n_mem * (n_mem - 1)) * spread)
    loss_ref[...] = jnp.zeros((8, 128), F32) + jnp.sum(cell)


def backward_kernel(
    ids, got0, got2, got1, got3, x_ref, hidden_ref, slope_ref, w_out_ref, bout_ref,
    keep_ref, send_ref, back, back_wide, small,
):
    mem_dev, sub, n_vars = got0.shape
    core = ids[2]
    hid = hidden_ref.shape[1]
    y = ids[0]
    for k, got in enumerate((got0, got1, got2, got3)):
        source = y ^ k
        for m in range(mem_dev):
            start = pl.multiple_of(m * 4 * sub + source * sub, sub)
            back[pl.ds(start, sub), :] = got[m]
    var = lax.broadcasted_iota(jnp.int32, (n_vars, 128), 0)
    lane = lax.broadcasted_iota(jnp.int32, (n_vars, 128), 1)
    place = jnp.where(lane == var + 3 * (var // PER_BLOCK), 1.0, 0.0).astype(BF16)
    back_wide[...] = jnp.dot(back[...], place, preferred_element_type=F32).astype(BF16)

    for start in range(0, hid, 256):
        cols = slice(start, start + 256)
        upward = jnp.dot(back[...], w_out_ref[:, cols], preferred_element_type=F32)
        dhidden = (upward * slope_ref[:, cols]).astype(BF16)
        small[:, cols] = lax.dot_general(
            back_wide[...], hidden_ref[:, cols], (((0,), (0,)), ((), ())), preferred_element_type=F32
        )
        small[ROW_BIN : ROW_BIN + 1, cols] = jnp.sum(dhidden.astype(F32), axis=0, keepdims=True)
        grad = lax.dot_general(
            x_ref[...], dhidden, (((0,), (0,)), ((), ())), preferred_element_type=F32
        )
        grad = grad.reshape(32, 2, 16, 256)
        first, second = grad[:, 0], grad[:, 1]
        keep_ref[:, :, cols] = jnp.where(core == 0, first, second)
        send_ref[:, :, cols] = jnp.where(core == 0, second, first).astype(BF16)

    small[ROW_BOUT : ROW_BOUT + 1, 0:n_vars] = bout_ref[...]
    half = hid // 2
    mine = pl.ds(pl.multiple_of(core * half, half), half)
    other = pl.ds(pl.multiple_of((1 - core) * half, half), half)
    for q in range(8):
        rows = small[16 * q : 16 * q + 16, mine]
        for t in range(4):
            keep_ref[4 * q + t, :, hid:] = rows[:, t * 128 : (t + 1) * 128]
        rows = unfold(small[16 * q : 16 * q + 16, other]).astype(BF16)
        for t in range(4):
            send_ref[4 * q + t, :, hid:] = rows[:, t * 128 : (t + 1) * 128]


def payload_kernel(keep_ref, got_ref, out_hbm, out_ref, sems):
    n_plane, _, width = keep_ref.shape
    hid = width - 128
    piece = n_plane // 4
    stores = []
    for i in range(4):
        part = slice(i * piece, (i + 1) * piece)
        total = keep_ref[part, :, 0:hid] + got_ref[part, :, 0:hid].astype(F32)
        out_ref[part, :, 0:hid] = total.astype(BF16)
        for j in range(i * piece, (i + 1) * piece):
            block = unfold(keep_ref[j, :, hid:] + fold(got_ref[j, :, hid:].astype(F32)))
            out_ref[j, :, hid:] = block.astype(BF16)
        part = pl.ds(i * piece, piece)
        store = pltpu.make_async_copy(out_ref.at[part], out_hbm.at[part], sems.at[i])
        store.start()
        stores.append(store)
    for store in stores:
        store.wait()


def plane_kernel(ids, landed_ref, own_ref, small_ref, part2, part1, part3):
    hid = own_ref.shape[1]
    total = jnp.sum(landed_ref[...].astype(F32), axis=0)
    small = fold(total[:, hid:])
    small_ref[...] = small
    zhi = ids[1]
    quarters = [total[4 * z : 4 * z + 4, 0:hid] for z in range(4)]

    def quarter(which):
        out = quarters[3]
        for z in range(3):
            out = jnp.where(which == z, quarters[z], out)
        return out

    own_ref[...] = quarter(zhi)
    for k, out in ((1, part1), (2, part2), (3, part3)):
        rows = quarter(lax.rem(zhi + k, 4))
        for j in range(4):
            out[4 * j : 4 * j + 4, 0:256] = rows[:, j * 256 : (j + 1) * 256]
        out[:, 256:384] = small


def total_kernel(ids, own_ref, small_ref, got2, got1, got3, loss_ref, grad_ref, copies_ref):
    zhi = ids[1]
    for j in range(4):
        acc = own_ref[:, j * 256 : (j + 1) * 256]
        for got in (got1, got2, got3):
            acc = acc + got[4 * j : 4 * j + 4, 0:256]
        grad_ref[:, j * 256 : (j + 1) * 256] = acc
    parts = [small_ref[...]] + [got[:, 256:384] for got in (got1, got2, got3)]
    acc = None
    for source in range(4):
        term = parts[0]
        for k in range(1, 4):
            term = jnp.where(lax.rem(zhi + 4 - k, 4) == source, parts[k], term)
        acc = term if acc is None else acc + term
    row = lax.broadcasted_iota(jnp.int32, acc.shape, 0)
    acc = jnp.where(row == ROW_LOSS, loss_ref[0:1, :], acc)
    copies_ref[...] = jnp.broadcast_to(acc[None], copies_ref.shape)


def small_half(blocks, full):
    for q in range(8):
        for t in range(4):
            full[16 * q : 16 * q + 16, t * 128 : (t + 1) * 128] = blocks[4 * q + t]


def plain_rows(full, out_ref, scale):
    n_vars = out_ref.shape[0]
    for q in range(8):
        count = min(PER_BLOCK, n_vars - PER_BLOCK * q)
        out_ref[PER_BLOCK * q : PER_BLOCK * q + count, :] = full[16 * q : 16 * q + count, :] * scale


def own_kernel(
    scale, ids, grad_ref, mine, in_hbm, out_hbm, bin_hbm, full, in_ref, out_ref, bin_ref, sems
):
    half = full.shape[1]
    cols = pl.ds(pl.multiple_of(ids[2] * half, half), half)
    in_ref[...] = grad_ref[...] * scale
    small_half(mine, full)
    plain_rows(full, out_ref, scale)
    bin_ref[...] = full[ROW_BIN : ROW_BIN + 1, :] * scale
    stores = [
        pltpu.make_async_copy(out_ref, out_hbm.at[:, cols], sems.at[0]),
        pltpu.make_async_copy(in_ref, in_hbm, sems.at[1]),
        pltpu.make_async_copy(bin_ref, bin_hbm.at[:, cols], sems.at[2]),
    ]
    for copy in stores:
        copy.start()
    for copy in stores:
        copy.wait()


def other_kernel(
    scale, loss_scale, ids, out_before, bin_before, mine, theirs,
    out_hbm, bin_hbm, bout_hbm, loss_hbm, full, out_ref, bin_ref, bout_ref, loss_ref, sems,
):
    core = ids[2]
    half = full.shape[1]
    n_vars = out_ref.shape[0]
    cols = pl.ds(pl.multiple_of((1 - core) * half, half), half)
    small_half(theirs, full)
    plain_rows(full, out_ref, scale)
    bin_ref[...] = full[ROW_BIN : ROW_BIN + 1, :] * scale
    row = ROW_BOUT - 112
    here, there = mine[28, row : row + 1, :], theirs[28, row : row + 1, :]
    bout_ref[...] = jnp.where(core == 0, here, there)[:, 0:n_vars] * scale
    totals = []
    for blocks in (mine, theirs):
        total = jnp.zeros((1, 128), F32)
        for n in range(blocks.shape[0]):
            total = total + blocks[n, ROW_LOSS : ROW_LOSS + 1, :]
        totals.append(total)
    loss_ref[...] = (totals[0] + totals[1])[:, 0:1] * loss_scale
    stores = [
        pltpu.make_async_copy(out_ref, out_hbm.at[:, cols], sems.at[0]),
        pltpu.make_async_copy(bin_ref, bin_hbm.at[:, cols], sems.at[1]),
        pltpu.make_async_copy(bout_ref, bout_hbm, sems.at[2]),
        pltpu.make_async_copy(loss_ref, loss_hbm, sems.at[3]),
    ]
    for copy in stores:
        copy.start()
    for copy in stores:
        copy.wait()


def per_device(latents, w_in, b_in, w_out, b_out, targets, area, var_weight, member_rank, obs_rank):
    mem_dev = latents.shape[1]
    pts_dev = latents.shape[2]
    width = latents.shape[3]
    hid = w_in.shape[1]
    n_vars = w_out.shape[1]
    n_y = lax.axis_size("y")
    n_mem = mem_dev * n_y
    sub = pts_dev // n_y
    rows = mem_dev * pts_dev
    n_points = pts_dev * lax.axis_size(GRID)
    scale = 1.0 / math.sqrt(lax.axis_size("zhi") * n_mem * n_points)
    ids = jnp.stack(
        [lax.axis_index("y"), lax.axis_index("zhi"), lax.axis_index("core")]
    ).astype(jnp.int32)
    shape = jax.ShapeDtypeStruct

    x = latents.reshape(rows, width)
    w_out_t = w_out.T
    ranks = member_rank[0].transpose(0, 2, 1)
    obs = obs_rank[0].T
    truth = targets[0].T
    sent = shape((mem_dev, sub, n_vars), BF16)
    whole = pl.BlockSpec(memory_space=pltpu.VMEM)

    hbm = pl.BlockSpec(memory_space=pltpu.HBM)
    operands = [
        pltpu.with_memory_space_constraint(arr, pltpu.HBM)
        for arr in (
            ranks, obs, area[None, :], var_weight[None, :],
            x, w_in, b_in[None, :], b_out[None, :],
        )
    ]
    w_in_hbm = operands[5]
    weight, bout, cot0, cot2, cot1, cot3, x, w_first, b_in, b_out = pl.pallas_call(
        cotangent_kernel,
        in_specs=[SMEM] + [hbm] * 8,
        out_specs=[whole] * 10,
        out_shape=[shape((sub, n_vars), F32), shape((1, n_vars), F32)]
        + [sent] * 4
        + [
            shape((rows, width), BF16),
            shape((width, hid // 2), BF16),
            shape((1, hid), F32),
            shape((1, n_vars), F32),
        ],
        scratch_shapes=[
            pltpu.VMEM((n_y, mem_dev, sub, n_vars), BF16),
            pltpu.VMEM((n_mem, sub, n_vars), jnp.int32),
            pltpu.VMEM((sub, n_vars), jnp.int32),
            pltpu.VMEM((1, sub), F32),
            pltpu.VMEM((1, n_vars), F32),
            pltpu.SemaphoreType.DMA((14,)),
        ],
        compiler_params=PARAMS,
        name="cotangent",
    )(ids, *operands)
    b_in_later, cot2, cot1, cot3 = lax.optimization_barrier((b_in, cot2, cot1, cot3))
    cot2 = lax.ppermute(cot2, "y", pairs_of("y", 2))
    cot1 = lax.ppermute(cot1, "y", pairs_of("y", 1))
    cot3 = lax.ppermute(cot3, "y", pairs_of("y", 3))

    cols = hid // 2
    by_cols = lambda height: pl.BlockSpec((height, cols), lambda i: (0, i))
    hidden, slope = pl.pallas_call(
        forward_kernel,
        grid=(hid // cols,),
        in_specs=[const_spec((rows, width)), const_spec((width, cols)), hbm, by_cols(1)],
        out_specs=[by_cols(rows), by_cols(rows)],
        out_shape=[shape((rows, hid), BF16), shape((rows, hid), F32)],
        scratch_shapes=[pltpu.VMEM((width, cols), BF16), pltpu.SemaphoreType.DMA],
        compiler_params=PARAMS,
        name="forward",
    )(x, w_first, w_in_hbm, b_in_later)

    n_plane = lax.axis_size(PLANE)
    block = width // (2 * n_plane)
    keep, send = pl.pallas_call(
        backward_kernel,
        in_specs=[SMEM] + [whole] * 9,
        out_specs=[whole] * 2,
        out_shape=[
            shape((n_plane, block, hid + 128), F32),
            shape((n_plane, block, hid + 128), BF16),
        ],
        scratch_shapes=[
            pltpu.VMEM((rows, n_vars), BF16),
            pltpu.VMEM((rows, 128), BF16),
            pltpu.VMEM((128, hid), F32),
        ],
        compiler_params=PARAMS,
        name="backward",
    )(ids, cot0, cot2, cot1, cot3, x, hidden, slope, w_out_t, bout)

    swap = [(0, 1), (1, 0)]
    got = lax.ppermute(send, "core", swap)
    payload_shape = (n_plane, block, hid + 128)
    payload = pl.pallas_call(
        payload_kernel,
        in_specs=[whole] * 2,
        out_specs=hbm,
        out_shape=shape(payload_shape, BF16),
        scratch_shapes=[pltpu.VMEM(payload_shape, BF16), pltpu.SemaphoreType.DMA((4,))],
        compiler_params=PARAMS,
        name="payload",
    )(keep, got)
    payload, hidden = lax.optimization_barrier((payload, hidden))
    landed = lax.all_to_all(payload, PLANE, 0, 0, tiled=True)
    val0, val2, val1, val3 = pl.pallas_call(
        forecast_kernel,
        in_specs=[SMEM] + [whole] * 3,
        out_specs=[whole] * 4,
        out_shape=[sent] * 4,
        scratch_shapes=[pltpu.VMEM((rows, n_vars), F32)],
        compiler_params=PARAMS,
        name="forecast",
    )(ids, hidden, w_out_t, b_out)
    val2 = lax.ppermute(val2, "y", pairs_of("y", 2))
    val1 = lax.ppermute(val1, "y", pairs_of("y", 1))
    val3 = lax.ppermute(val3, "y", pairs_of("y", 3))
    part_loss = pl.pallas_call(
        loss_kernel,
        in_specs=[whole] * 6,
        out_specs=whole,
        out_shape=shape((8, 128), F32),
        compiler_params=PARAMS,
        name="loss",
    )(val0, val2, val1, val3, truth, weight)

    part = shape((block, 384), F32)
    own, small, part2, part1, part3 = pl.pallas_call(
        plane_kernel,
        in_specs=[SMEM, whole],
        out_specs=[whole] * 5,
        out_shape=[shape((block // 4, hid), F32), shape((block, 128), F32), part, part, part],
        compiler_params=PARAMS,
        name="plane_sum",
    )(ids, landed)
    part2 = lax.ppermute(part2, "zhi", shift("zhi", 2))
    part1 = lax.ppermute(part1, "zhi", shift("zhi", 1))
    part3 = lax.ppermute(part3, "zhi", shift("zhi", 3))
    grad_in, copies = pl.pallas_call(
        total_kernel,
        in_specs=[SMEM] + [whole] * 6,
        out_specs=[whole] * 2,
        out_shape=[shape((block // 4, hid), F32), shape((n_plane, block, 128), F32)],
        compiler_params=PARAMS,
        name="total",
    )(ids, own, small, part2, part1, part3, part_loss)

    mine = lax.all_to_all(copies, PLANE, 0, 0, tiled=True)
    theirs = lax.ppermute(mine, "core", swap)
    half = hid // 2
    in_shape = shape((block // 4, hid), F32)
    out_shape = shape((n_vars, hid), F32)
    bin_shape = shape((1, hid), F32)
    bout_shape = shape((1, n_vars), F32)
    loss_shape = shape((1, 1), F32)
    grad_in, grad_out, grad_bin = pl.pallas_call(
        lambda *refs: own_kernel(scale, *refs),
        in_specs=[SMEM] + [whole] * 2,
        out_specs=[hbm] * 3,
        out_shape=[in_shape, out_shape, bin_shape],
        scratch_shapes=[
            pltpu.VMEM((128, half), F32),
            pltpu.VMEM(in_shape.shape, F32),
            pltpu.VMEM((n_vars, half), F32),
            pltpu.VMEM((1, half), F32),
            pltpu.SemaphoreType.DMA((3,)),
        ],
        compiler_params=PARAMS,
        name="unpack_own",
    )(ids, grad_in, mine)
    grad_out, grad_bin, grad_bout, loss = pl.pallas_call(
        lambda *refs: other_kernel(scale, 1.0 / (n_points * n_vars), *refs),
        in_specs=[SMEM, hbm, hbm] + [whole] * 2,
        out_specs=[hbm] * 4,
        out_shape=[out_shape, bin_shape, bout_shape, loss_shape],
        input_output_aliases={1: 0, 2: 1},
        scratch_shapes=[
            pltpu.VMEM((128, half), F32),
            pltpu.VMEM((n_vars, half), F32),
            pltpu.VMEM((1, half), F32),
            pltpu.VMEM(bout_shape.shape, F32),
            pltpu.VMEM(loss_shape.shape, F32),
            pltpu.SemaphoreType.DMA((4,)),
        ],
        compiler_params=PARAMS,
        name="unpack_other",
    )(ids, grad_out, grad_bin, mine, theirs)
    return (loss.reshape(1), grad_in, grad_out.T, grad_bin.reshape(hid), grad_bout.reshape(n_vars))


def solution(mesh):
    split = Mesh(mesh.devices.reshape(4, 2, 4, 2, 4), NAMES)
    points = GRID + ("y",)
    in_specs = (
        P("zhi", "y", GRID, None),
        P(),
        P(),
        P(),
        P(),
        P("zhi", None, points),
        P(points),
        P(),
        P("zhi", None, None, points),
        P("zhi", None, points),
    )
    out_specs = (P("zhi"), P(NAMES, None), P(), P(), P())
    return jax.shard_map(
        per_device, mesh=split, in_specs=in_specs, out_specs=out_specs, check_vma=False
    )
```
